256 devices in a mesh: row: 8 (over x, core), col: 32 (over y, z).
Axes of the slice: x: 4, y: 4, z: 8, core: 2. Of those that a mesh axis runs over, the one named last changes fastest.
Arguments:
- normal: float32 [16384, 16384], P('row', 'col'), may hold values from -0.25 to 7.25, as said below
- jacobian: bfloat16 [512, 16384], P(None, ('row', 'col')), may hold values from -1 to 1
Outputs:
- updated: float32 [16384, 16384], P('row', 'col')
- panel: float32 [16384, 512], P('row', 'col')
The draws below stay inside these ranges and needn't reach their ends.
Inputs may be any that keep to these rules, and one draw needn't show every extreme that they name: `normal`: in logical order of rows and columns the matrix is symmetric and positive definite.
All inputs are finite; a program needn't handle non-finite values.
Results may differ from the reference program's by a relative error of at most 0.00035.
Values may be sent and summed in bfloat16 or wider, within the bound.
No kernel may reach another device: no remote copies, remote signals or barrier semaphores. Data moves between devices by JAX's collectives and lax.ppermute only.
A program may use at most 128 MiB of HBM per device.

```python
import math
import jax
import jax.numpy as jnp
from jax import lax

N = 16384
PW = 512
NB = 16
K = 512
N_ROW = 8
N_COL = 32


def logical_of_drawn(stored, part_count):
    span_len = N // part_count
    device_idx = stored // span_len
    within = stored % span_len
    return (within // NB * part_count + device_idx) * NB + within % NB


def draw_normal(key, part):
    key = jax.random.fold_in(key, 7)
    first_key, second_key = jax.random.split(key)
    base = jnp.clip(jax.random.normal(first_key, (N, N), jnp.float32), -2.0, 2.0)
    matrix = (base + base.T) * (1.0 / math.sqrt(N))
    diag_add = jax.random.uniform(second_key, (N,), jnp.float32, 4.0, 7.0)
    matrix = matrix + jnp.diag(diag_add)
    index_all = jnp.arange(N, dtype=jnp.int32)
    matrix = jnp.take(matrix, logical_of_drawn(index_all, N_ROW).astype(jnp.int32), axis=0)
    return jnp.take(matrix, logical_of_drawn(index_all, N_COL).astype(jnp.int32), axis=1)


def block_levels(own_key, dims, cuts, least, top_value):
    loudness = 1.0
    for dim, shards_of in cuts:
        draws = jax.random.uniform(jax.random.fold_in(jax.random.fold_in(own_key, 6), dim), (shards_of,), jnp.float32, least / len(cuts), top_value / len(cuts))
        loudness = loudness * jnp.repeat(jnp.exp(draws), dims[dim] // shards_of).reshape((-1,) + (1,) * (len(dims) - 1 - dim))
    return loudness


def centred(rng, shape, deviation, reach, cuts=(), held_as=jnp.bfloat16):
    drawn = deviation * jax.random.normal(rng, shape, jnp.float32)
    if cuts:
        drawn = drawn * block_levels(rng, shape, cuts, -0.22, 0.18)
    return jnp.clip(drawn, -reach, reach).astype(held_as)


def setup_inputs(seed: int = 0) -> dict:
    streams_of = jax.random.split(jax.random.key(seed), 3)
    return {
        "normal": draw_normal(jax.random.fold_in(streams_of[2], 71), 0),
        "jacobian": centred(streams_of[1], (K, N), (K // 16) ** -0.5, 1.0, ((1, 256),)),
    }


def stored_at(logical, part_count):
    tile_idx = logical // NB
    offset = logical % NB
    return tile_idx % part_count * (N // part_count) + tile_idx // part_count * NB + offset

def logical_of(stored, part_count):
    span_len = N // part_count
    device_idx = stored // span_len
    within = stored % span_len
    return (within // NB * part_count + device_idx) * NB + within % NB

def reference(normal, jacobian):
    index_all = jnp.arange(N, dtype=jnp.int32)
    col_rows = stored_at(logical_of(index_all, N_COL), N_ROW).astype(jnp.int32)
    jac_cols = jnp.take(jacobian, col_rows, axis=1)
    gram = normal + lax.dot_general(jacobian.astype(jnp.float32), jac_cols.astype(jnp.float32), (((0,), (0,)), ((), ())), preferred_element_type=jnp.float32)
    pivots = jnp.arange(PW, dtype=jnp.int32)
    pivot_rows = stored_at(pivots, N_ROW).astype(jnp.int32)
    pivot_cols = stored_at(pivots, N_COL).astype(jnp.int32)
    block = jnp.take(jnp.take(gram, pivot_rows, axis=0), pivot_cols, axis=1)
    factor = jnp.linalg.cholesky(block)
    inverse = jax.scipy.linalg.solve_triangular(factor, jnp.eye(PW, dtype=jnp.float32), lower=True)
    panel = jnp.dot(jnp.take(gram, pivot_cols, axis=1).astype(jnp.float32), inverse.T.astype(jnp.float32), precision=lax.Precision.HIGHEST, preferred_element_type=jnp.float32)
    far_rows = jnp.take(panel, col_rows, axis=0)
    updated = gram - lax.dot_general(panel.astype(jnp.float32), far_rows.astype(jnp.float32), (((1,), (1,)), ((), ())), precision=lax.Precision.HIGHEST, preferred_element_type=jnp.float32)
    return (updated, panel)
```

```python
import functools

import jax
import jax.numpy as jnp
from jax import lax
from jax.experimental import pallas as pl
from jax.experimental.pallas import tpu as pltpu
from jax.sharding import Mesh
from jax.sharding import PartitionSpec as P

PW = 512
NB = 16
T = 128
AXES = ("x", "core", "y", "z")
F32 = jnp.float32
BF16 = jnp.bfloat16
HI = lax.Precision.HIGHEST
VMEM = pltpu.VMEM


def nt(a, b, precision=None):
    return lax.dot_general(a, b, (((1,), (1,)), ((), ())), precision=precision, preferred_element_type=F32)


def nn(a, b, precision=None):
    return lax.dot_general(a, b, (((1,), (0,)), ((), ())), precision=precision, preferred_element_type=F32)


def tn(a, b):
    return lax.dot_general(a, b, (((0,), (0,)), ((), ())), preferred_element_type=F32)


def split(x):
    high = x.astype(BF16)
    return high, (x - high.astype(F32)).astype(BF16)


def prep_kernel(cols_ref, rows_ref, jac_ref, wide_ref, corner_ref, near_ref):
    cols = cols_ref[...].T[:NB]
    high, low = split(cols)
    for q in range(4):
        wide_ref[q] = high[:, q * PW : (q + 1) * PW]
        wide_ref[4 + q] = low[:, q * PW : (q + 1) * PW]
        wide_ref[8 + q] = jac_ref[q * NB : (q + 1) * NB, :]
    corner = jnp.concatenate([cols[:8, :64], cols[8:, :64]], axis=1)
    first, rest = split(corner)
    rest = corner - first.astype(F32)
    second = rest.astype(BF16)
    third = (rest - second.astype(F32)).astype(BF16)
    corner_ref[:, :T] = jnp.concatenate([first.astype(F32), second.astype(F32)], axis=0).astype(BF16)
    corner_ref[:, T:] = jnp.concatenate([third.astype(F32), jnp.zeros((8, T), F32)], axis=0).astype(BF16)
    high, low = split(rows_ref[...])
    for i in range(4):
        near_ref[i, :, :PW] = high[i * NB : (i + 1) * NB]
        near_ref[i, :, PW:] = low[i * NB : (i + 1) * NB]


def prep(normal, jac_t):
    rows = normal.shape[0]
    whole = pl.BlockSpec(memory_space=VMEM)
    return pl.pallas_call(
        prep_kernel,
        grid=(1,),
        in_specs=[
            pl.BlockSpec((rows, T), lambda i: (0, 0)),
            pl.BlockSpec((64, PW), lambda i: (0, 0)),
            pl.BlockSpec((64, PW), lambda i: (0, 0)),
        ],
        out_specs=[
            pl.BlockSpec((12, NB, PW), lambda i: (0, 0, 0)),
            pl.BlockSpec((NB, 2 * T), lambda i: (0, 0)),
            pl.BlockSpec((4, NB, 2 * PW), lambda i: (0, 0, 0)),
        ],
        out_shape=[
            jax.ShapeDtypeStruct((12, NB, PW), BF16),
            jax.ShapeDtypeStruct((NB, 2 * T), BF16),
            jax.ShapeDtypeStruct((4, NB, 2 * PW), BF16),
        ],
        compiler_params=pltpu.CompilerParams(vmem_limit_bytes=24 << 20),
    )(normal, normal, jac_t)


def factor_tile(tile):
    q = 8
    groups = T // q
    rows = [tile[q * i : q * (i + 1), :] for i in range(groups)]
    lane = lax.broadcasted_iota(jnp.int32, (q, T), 1)
    out = []
    spread = lambda v: jnp.broadcast_to(v, (q, T))
    for g in range(groups):
        base = g * q
        cols = {i: [spread(rows[i][:, base + l : base + l + 1]) for l in range(q)] for i in range(g, groups)}
        low = [[None] * q for _ in range(q)]
        inv = [[None] * q for _ in range(q)]
        pivot = [[spread(cols[g][l][k : k + 1, :]) if k >= l else None for l in range(q)] for k in range(q)]
        for j in range(q):
            d = pivot[j][j]
            for m in range(j):
                d = d - low[j][m] * low[j][m]
            r = lax.rsqrt(d)
            inv[j][j] = r
            for i in range(j + 1, q):
                t = pivot[i][j]
                for m in range(j):
                    t = t - low[i][m] * low[j][m]
                low[i][j] = t * r
        for i in range(q):
            for j in range(i):
                t = low[i][j] * inv[j][j]
                for m in range(j + 1, i):
                    t = t + low[i][m] * inv[m][j]
                inv[i][j] = -(t * inv[i][i])
        inside = (lane >= base) & (lane < base + q)
        top = [
            jnp.where(inside, jnp.where(lane == base + l, 1.0, 0.0), spread(rows[g][l : l + 1, :])) for l in range(q)
        ]
        done = []
        for k in range(q):
            t = inv[k][0] * top[0]
            for l in range(1, k + 1):
                t = t + inv[k][l] * top[l]
            done.append(t)
        weight = []
        for k in range(q):
            t = inv[k][k] * done[k]
            for l in range(k + 1, q):
                t = t + inv[l][k] * done[l]
            weight.append(t)
        sub = lax.broadcasted_iota(jnp.int32, (q, T), 0)
        mine = done[0]
        for k in range(1, q):
            mine = jnp.where(sub >= k, done[k], mine)
        out.append(jnp.where(lane < base + q, mine, 0.0))
        for i in range(g + 1, groups):
            acc = cols[i][0] * weight[0]
            for k in range(1, q):
                acc = acc + cols[i][k] * weight[k]
            rows[i] = jnp.where(inside, 0.0, rows[i]) - acc
    return jnp.concatenate(out, 0)


def factor(work, inv):
    inv[...] = jnp.zeros_like(inv)
    tiles = PW // T
    for b in range(tiles):
        lo, hi = b * T, (b + 1) * T
        here = factor_tile(work[lo:hi, lo:hi])
        inv[lo:hi, lo:hi] = here
        if b:
            inv[lo:hi, :lo] = nn(here, inv[lo:hi, :lo], HI)
        if b < tiles - 1:
            below = nt(work[hi:, lo:hi], here, HI)
            work[hi : hi + T, hi : hi + T] -= nt(below[:T], below[:T], HI)
            if b < tiles - 2:
                work[hi + T :, hi:] -= nt(below[T:], below, HI)
            inv[hi:, :hi] -= nn(below, inv[lo:hi, :hi], HI)


def block_kernel(
    core_ref, own_ref, other_ref, inv_hi, inv_lo, far_hi, far_lo, jac_first, jac_cols, work, inv, gram, pieces, thirds
):
    core = core_ref[0]
    for x in range(4):
        for ref, r in ((own_ref, 2 * x + core), (other_ref, 2 * x + 1 - core)):
            for a in range(4):
                at = pl.ds(pl.multiple_of(a * T + r * NB, NB), NB)
                jac_first[at, :] = ref[x, a, :, :PW]
                jac_cols[at, :] = ref[x, a, :, 5 * PW : 6 * PW]
                gram[at, :] = ref[x, a, :, 6 * PW : 7 * PW].astype(F32) + ref[x, a, :, 7 * PW :].astype(F32)
                for z in range(8):
                    row = (a * 8 + z) * NB
                    lanes = pl.ds(pl.multiple_of(r * T, T), T)
                    start = PW + z * 2 * T
                    pieces[row : row + NB, lanes] = ref[x, a, :, start : start + T]
                    thirds[row : row + NB, lanes] = ref[x, a, :, start + T : start + 2 * T]
    src = lax.broadcasted_iota(jnp.int32, (8 * T, PW), 0)
    dst = lax.broadcasted_iota(jnp.int32, (8 * T, PW), 1)
    to = (src // 16 % 4) * T + (src // T) * NB + src % NB
    for half in range(2):
        place = jnp.where((to == dst) & (src // 64 % 2 == half), 1.0, 0.0).astype(BF16)
        a = nn(pieces[...], place).reshape(32, 2, 8, PW)
        b = nn(thirds[...], place).reshape(32, 2, 8, PW)
        work.reshape(32, 2, 8, PW)[:, half] = a[:, 0] + a[:, 1] + b[:, 0]
    first = jac_first[...]
    work[...] += nt(first, first)
    gram[...] += nt(first, jac_cols[...])
    factor(work, inv)
    high, low = split(inv[...])
    inv_hi[...] = high
    inv_lo[...] = low
    high, low = split(nn(inv[...], gram[...], HI))
    far_hi[...] = high
    far_lo[...] = low


def block(core, own, other):
    whole = pl.BlockSpec(memory_space=VMEM)
    return pl.pallas_call(
        block_kernel,
        in_specs=[pl.BlockSpec(memory_space=pltpu.SMEM), whole, whole],
        out_specs=[whole] * 6,
        out_shape=[jax.ShapeDtypeStruct((PW, PW), BF16)] * 6,
        scratch_shapes=[
            VMEM((PW, PW), F32),
            VMEM((PW, PW), F32),
            VMEM((PW, PW), F32),
            VMEM((PW, 8 * T), BF16),
            VMEM((PW, 8 * T), BF16),
        ],
        compiler_params=pltpu.CompilerParams(vmem_limit_bytes=40 << 20),
    )(core, own, other)


def last_kernel(
    col_ref, normal_ref, high_ref, low_ref, jac_ref, inv_hi, inv_lo, far_hi, far_lo, first, cols, out_ref, panel_ref, save
):
    rows = jac_ref[...].reshape(PW, PW)
    panel_in = high_ref[...].reshape(PW, PW).astype(F32) + low_ref[...].reshape(PW, PW).astype(F32)
    panel_in = panel_in + nt(first[...], rows)
    high, low = split(panel_in)
    panel = nn(inv_hi[...], high) + (nn(inv_lo[...], high) + nn(inv_hi[...], low))
    save[...] = panel
    panel_ref[...] = save[pl.ds(pl.multiple_of(col_ref[0] * NB, NB), NB), :]
    high, low = split(panel)
    drop = tn(high, far_hi[...]) + (tn(low, far_hi[...]) + tn(high, far_lo[...]))
    out_ref[...] = normal_ref[...] + nt(rows, cols[...]) - drop


def last(col, normal, wide, inv_hi, inv_lo, far_hi, far_lo, first, cols):
    rows = normal.shape[0]
    whole = pl.BlockSpec((PW, PW), lambda q: (0, 0))
    return pl.pallas_call(
        last_kernel,
        grid=(rows // PW,),
        in_specs=[
            pl.BlockSpec(memory_space=pltpu.SMEM),
            pl.BlockSpec((PW, PW), lambda q: (q, 0)),
            pl.BlockSpec((32, 1, NB, PW), lambda q: (0, q, 0, 0)),
            pl.BlockSpec((32, 1, NB, PW), lambda q: (0, 4 + q, 0, 0)),
            pl.BlockSpec((8, 4, NB, PW), lambda q: (q, 2, 0, 0)),
        ]
        + [whole] * 6,
        out_specs=[
            pl.BlockSpec((PW, PW), lambda q: (q, 0)),
            pl.BlockSpec((NB, PW), lambda q: (0, q)),
        ],
        out_shape=[
            jax.ShapeDtypeStruct((rows, PW), F32),
            jax.ShapeDtypeStruct((NB, rows), F32),
        ],
        scratch_shapes=[VMEM((PW, PW), F32)],
        compiler_params=pltpu.CompilerParams(vmem_limit_bytes=40 << 20),
    )(col, normal, wide, wide, wide, inv_hi, inv_lo, far_hi, far_lo, first, cols)


def position(r, y, z):
    return (r * 4 + y) * 8 + z


def spread_over(value, axis, count):
    return lax.all_to_all(jnp.broadcast_to(value[None], (count,) + value.shape), axis, 0, 0, tiled=True)


def per_device(normal, jacobian):
    core = lax.axis_index("core").astype(jnp.int32)[None]
    col = (lax.axis_index("y") * 8 + lax.axis_index("z")).astype(jnp.int32)[None]
    jac_t = jacobian.T
    wide, corner, near = prep(normal, jac_t)
    wide = lax.all_gather(wide, ("y", "z"), axis=0, tiled=False)
    tiles = lax.all_to_all(jac_t.reshape(4, NB, PW), "y", 0, 0, tiled=True)
    swap = [(position(r, y, z), position(z, y, r)) for r in range(8) for y in range(4) for z in range(8)]
    swapped = lax.ppermute(tiles, AXES, swap)
    got = spread_over(jnp.concatenate([tiles[0], corner], axis=1), "z", 8)
    sent = jnp.concatenate([got[0, :, :PW]] + [got[z, :, PW:] for z in range(8)], axis=1)
    got = spread_over(sent, "y", 4)
    sent = jnp.concatenate([got, swapped, near], axis=2)
    own = spread_over(sent, "x", 4)
    flip = [(position(r, y, z), position(r ^ 1, y, z)) for r in range(8) for y in range(4) for z in range(8)]
    other = lax.ppermute(own, AXES, flip)
    parts = block(core, own, other)
    updated, panel_t = last(col, normal, wide, *parts)
    return updated, panel_t.T


def solution(mesh):
    fine = Mesh(mesh.devices.reshape(4, 2, 4, 8), AXES)
    rows, cols = ("x", "core"), ("y", "z")
    return jax.shard_map(
        per_device,
        mesh=fine,
        in_specs=(P(rows, cols), P(None, AXES)),
        out_specs=(P(rows, cols), P(rows, cols)),
        check_vma=False,
    )
```

```python
import functools

import jax
import jax.numpy as jnp
from jax import lax
from jax.experimental import pallas as pl
from jax.experimental.pallas import tpu as pltpu
from jax.sharding import Mesh
from jax.sharding import PartitionSpec as P

PW = 512
NB = 16
T = 128
AXES = ("x", "core", "y", "z")
F32 = jnp.float32
BF16 = jnp.bfloat16
HI = lax.Precision.HIGHEST
VMEM = pltpu.VMEM


def nt(a, b, precision=None):
    return lax.dot_general(a, b, (((1,), (1,)), ((), ())), precision=precision, preferred_element_type=F32)


def nn(a, b, precision=None):
    return lax.dot_general(a, b, (((1,), (0,)), ((), ())), precision=precision, preferred_element_type=F32)


def tn(a, b):
    return lax.dot_general(a, b, (((0,), (0,)), ((), ())), preferred_element_type=F32)


def split(x):
    high = x.astype(BF16)
    return high, (x - high.astype(F32)).astype(BF16)


def prep_kernel(cols_ref, rows_ref, jac_ref, wide_ref, corner_ref, near_ref):
    cols = cols_ref[...].T[:NB]
    high, low = split(cols)
    for q in range(4):
        wide_ref[q] = high[:, q * PW : (q + 1) * PW]
        wide_ref[4 + q] = low[:, q * PW : (q + 1) * PW]
        wide_ref[8 + q] = jac_ref[q * NB : (q + 1) * NB, :]
    corner_ref[...] = jnp.concatenate([cols[:8, :64], cols[8:, :64]], axis=1)
    high, low = split(rows_ref[...])
    for i in range(4):
        near_ref[i, :, :PW] = high[i * NB : (i + 1) * NB]
        near_ref[i, :, PW:] = low[i * NB : (i + 1) * NB]


def prep(normal, jac_t):
    rows = normal.shape[0]
    return pl.pallas_call(
        prep_kernel,
        grid=(1,),
        in_specs=[
            pl.BlockSpec((rows, T), lambda i: (0, 0)),
            pl.BlockSpec((64, PW), lambda i: (0, 0)),
            pl.BlockSpec((64, PW), lambda i: (0, 0)),
        ],
        out_specs=[
            pl.BlockSpec((12, NB, PW), lambda i: (0, 0, 0)),
            pl.BlockSpec((8, T), lambda i: (0, 0)),
            pl.BlockSpec((4, NB, 2 * PW), lambda i: (0, 0, 0)),
        ],
        out_shape=[
            jax.ShapeDtypeStruct((12, NB, PW), BF16),
            jax.ShapeDtypeStruct((8, T), F32),
            jax.ShapeDtypeStruct((4, NB, 2 * PW), BF16),
        ],
        compiler_params=pltpu.CompilerParams(vmem_limit_bytes=62 << 20),
    )(normal, normal, jac_t)


def factor_tile(tile):
    q = 8
    groups = T // q
    rows = [tile[q * i : q * (i + 1), :] for i in range(groups)]
    lane = lax.broadcasted_iota(jnp.int32, (q, T), 1)
    out = []
    spread = lambda v: jnp.broadcast_to(v, (q, T))
    for g in range(groups):
        base = g * q
        cols = {i: [spread(rows[i][:, base + l : base + l + 1]) for l in range(q)] for i in range(g, groups)}
        low = [[None] * q for _ in range(q)]
        inv = [[None] * q for _ in range(q)]
        pivot = [[spread(cols[g][l][k : k + 1, :]) if k >= l else None for l in range(q)] for k in range(q)]
        for j in range(q):
            d = pivot[j][j]
            for m in range(j):
                d = d - low[j][m] * low[j][m]
            r = lax.rsqrt(d)
            inv[j][j] = r
            for i in range(j + 1, q):
                t = pivot[i][j]
                for m in range(j):
                    t = t - low[i][m] * low[j][m]
                low[i][j] = t * r
        for i in range(q):
            for j in range(i):
                t = low[i][j] * inv[j][j]
                for m in range(j + 1, i):
                    t = t + low[i][m] * inv[m][j]
                inv[i][j] = -(t * inv[i][i])
        inside = (lane >= base) & (lane < base + q)
        top = [
            jnp.where(inside, jnp.where(lane == base + l, 1.0, 0.0), spread(rows[g][l : l + 1, :])) for l in range(q)
        ]
        done = []
        for k in range(q):
            t = inv[k][0] * top[0]
            for l in range(1, k + 1):
                t = t + inv[k][l] * top[l]
            done.append(t)
        weight = []
        for k in range(q):
            t = inv[k][k] * done[k]
            for l in range(k + 1, q):
                t = t + inv[l][k] * done[l]
            weight.append(t)
        sub = lax.broadcasted_iota(jnp.int32, (q, T), 0)
        mine = done[0]
        for k in range(1, q):
            mine = jnp.where(sub >= k, done[k], mine)
        out.append(jnp.where(lane < base + q, mine, 0.0))
        for i in range(g + 1, groups):
            acc = cols[i][0] * weight[0]
            for k in range(1, q):
                acc = acc + cols[i][k] * weight[k]
            rows[i] = jnp.where(inside, 0.0, rows[i]) - acc
    return jnp.concatenate(out, 0)


def factor(work, inv):
    inv[...] = jnp.zeros_like(inv)
    tiles = PW // T
    for b in range(tiles):
        lo, hi = b * T, (b + 1) * T
        here = factor_tile(work[lo:hi, lo:hi])
        inv[lo:hi, lo:hi] = here
        if b:
            inv[lo:hi, :lo] = nn(here, inv[lo:hi, :lo], HI)
        if b < tiles - 1:
            below = nt(work[hi:, lo:hi], here, HI)
            work[hi : hi + T, hi : hi + T] -= nt(below[:T], below[:T], HI)
            if b < tiles - 2:
                work[hi + T :, hi:] -= nt(below[T:], below, HI)
            inv[hi:, :hi] -= nn(below, inv[lo:hi, :hi], HI)


def place(refs, core, store):
    for x in range(4):
        for ref, r in ((refs[0], 2 * x + core), (refs[1], 2 * x + 1 - core)):
            for a in range(4):
                store(ref, x, a, r)


def tile_rows(a, r):
    return pl.ds(pl.multiple_of(a * T + r * NB, NB), NB)


def block_kernel(core_ref, own_ref, other_ref, inv_ref, first_ref, work, pieces):
    core = core_ref[0]

    def store(ref, x, a, r):
        upper, lower = ref[x, a, :, :PW], ref[x, a, :, PW : 2 * PW]
        first_ref[tile_rows(a, r), :] = jnp.concatenate([upper, lower], axis=0).astype(BF16)
        lanes = pl.ds(pl.multiple_of(r * T, T), T)
        for z in range(8):
            start = 2 * PW + z * T
            pieces[(a * 8 + z) * 8 : (a * 8 + z + 1) * 8, lanes] = ref[x, a, :, start : start + T]

    place((own_ref, other_ref), core, store)
    src = lax.broadcasted_iota(jnp.int32, (8 * T, PW), 0)
    dst = lax.broadcasted_iota(jnp.int32, (8 * T, PW), 1)
    to = (src // 16 % 4) * T + (src // T) * NB + src % NB
    high, rest = split(pieces[...])
    rest = pieces[...] - high.astype(F32)
    middle, low = split(rest)
    for half in range(2):
        move = jnp.where((to == dst) & (src // 64 % 2 == half), 1.0, 0.0).astype(BF16)
        part = nn(high, move) + nn(middle, move) + nn(low, move)
        work.reshape(32, 2, 8, PW)[:, half] = part.reshape(32, 8, PW)
    first = first_ref[...]
    work[...] += nt(first, first)
    factor(work, inv_ref)


def block(core, own, other):
    whole = pl.BlockSpec(memory_space=VMEM)
    return pl.pallas_call(
        block_kernel,
        in_specs=[pl.BlockSpec(memory_space=pltpu.SMEM), whole, whole],
        out_specs=[whole] * 2,
        out_shape=[jax.ShapeDtypeStruct((PW, PW), F32), jax.ShapeDtypeStruct((PW, PW), BF16)],
        scratch_shapes=[VMEM((PW, PW), F32), VMEM((256, 8 * T), F32)],
        compiler_params=pltpu.CompilerParams(vmem_limit_bytes=62 << 20),
    )(core, own, other)


def far_kernel(place_ref, inv_ref, first_ref, near0, near1, near2, near3, inv_hi, inv_lo, far_hi, far_lo, cols, gram):
    core = place_ref[0]
    for k, near in enumerate((near0, near1, near2, near3)):
        x = lax.rem(place_ref[1] + 4 - k, 4)
        for side in range(2):
            r = 2 * x + (core if side == 0 else 1 - core)
            for a in range(4):
                at = tile_rows(a, r)
                cols[at, :] = near[side, a, :, :PW]
                gram[at, :] = near[side, a, :, PW : 2 * PW].astype(F32) + near[side, a, :, 2 * PW :].astype(F32)
    high, low = split(inv_ref[...])
    inv_hi[...] = high
    inv_lo[...] = low
    high, low = split(nn(inv_ref[...], gram[...] + nt(first_ref[...], cols[...]), HI))
    far_hi[...] = high
    far_lo[...] = low


def far(where, inv, first, near):
    whole = pl.BlockSpec(memory_space=VMEM)
    return pl.pallas_call(
        far_kernel,
        in_specs=[pl.BlockSpec(memory_space=pltpu.SMEM)] + [whole] * 6,
        out_specs=[whole] * 5,
        out_shape=[jax.ShapeDtypeStruct((PW, PW), BF16)] * 5,
        scratch_shapes=[VMEM((PW, PW), F32)],
        compiler_params=pltpu.CompilerParams(vmem_limit_bytes=62 << 20),
    )(where, inv, first, *near)


def last_kernel(
    col_ref, normal_ref, high_ref, low_ref, jac_ref, inv_hi, inv_lo, far_hi, far_lo, first, cols, out_ref, panel_ref, save
):
    rows = jac_ref[...].reshape(PW, PW)
    panel_in = high_ref[...].reshape(PW, PW).astype(F32) + low_ref[...].reshape(PW, PW).astype(F32)
    panel_in = panel_in + nt(first[...], rows)
    high, low = split(panel_in)
    panel = nn(inv_hi[...], high) + (nn(inv_lo[...], high) + nn(inv_hi[...], low))
    save[...] = panel
    panel_ref[...] = save[pl.ds(pl.multiple_of(col_ref[0] * NB, NB), NB), :]
    high, low = split(panel)
    drop = tn(high, far_hi[...]) + (tn(low, far_hi[...]) + tn(high, far_lo[...]))
    out_ref[...] = normal_ref[...] + nt(rows, cols[...]) - drop


def last(col, normal, wide, inv_hi, inv_lo, far_hi, far_lo, first, cols):
    rows = normal.shape[0]
    whole = pl.BlockSpec((PW, PW), lambda q: (0, 0))
    return pl.pallas_call(
        last_kernel,
        grid=(rows // PW,),
        in_specs=[
            pl.BlockSpec(memory_space=pltpu.SMEM),
            pl.BlockSpec((PW, PW), lambda q: (q, 0)),
            pl.BlockSpec((32, 1, NB, PW), lambda q: (0, q, 0, 0)),
            pl.BlockSpec((32, 1, NB, PW), lambda q: (0, 4 + q, 0, 0)),
            pl.BlockSpec((8, 4, NB, PW), lambda q: (q, 2, 0, 0)),
        ]
        + [whole] * 6,
        out_specs=[
            pl.BlockSpec((PW, PW), lambda q: (q, 0)),
            pl.BlockSpec((NB, PW), lambda q: (0, q)),
        ],
        out_shape=[
            jax.ShapeDtypeStruct((rows, PW), F32),
            jax.ShapeDtypeStruct((NB, rows), F32),
        ],
        scratch_shapes=[VMEM((PW, PW), F32)],
        compiler_params=pltpu.CompilerParams(vmem_limit_bytes=62 << 20),
    )(col, normal, wide, wide, wide, inv_hi, inv_lo, far_hi, far_lo, first, cols)


def position(r, y, z):
    return (r * 4 + y) * 8 + z


def spread_over(value, axis, count):
    return lax.all_to_all(jnp.broadcast_to(value[None], (count,) + value.shape), axis, 0, 0, tiled=True)


def moves(to):
    return [(position(r, y, z), position(*to(r, y, z))) for r in range(8) for y in range(4) for z in range(8)]


def per_device(normal, jacobian):
    core, x = lax.axis_index("core").astype(jnp.int32), lax.axis_index("x").astype(jnp.int32)
    where = jnp.stack([core, x])
    col = (lax.axis_index("y") * 8 + lax.axis_index("z")).astype(jnp.int32)[None]
    jac_t = jacobian.T
    wide, corner, near = prep(normal, jac_t)
    wide = lax.all_gather(wide, ("y", "z"), axis=0, tiled=False)
    tiles = lax.all_to_all(jac_t.reshape(4, NB, PW), "y", 0, 0, tiled=True)
    swapped = lax.ppermute(tiles, AXES, moves(lambda r, y, z: (z, y, r)))
    flip = moves(lambda r, y, z: (r ^ 1, y, z))
    near = jnp.concatenate([swapped, near], axis=2)
    near = jnp.stack([near, lax.ppermute(near, AXES, flip)])
    head = tiles[0].astype(F32)
    got = spread_over(jnp.concatenate([head[:8], head[8:], corner], axis=1), "z", 8)
    sent = jnp.concatenate([got[0, :, : 2 * PW]] + [got[z, :, 2 * PW :] for z in range(8)], axis=1)
    got = spread_over(sent, "y", 4)
    own = spread_over(got, "x", 4)
    other = lax.ppermute(own, AXES, flip)
    nears = [near] + [lax.ppermute(near, AXES, moves(lambda r, y, z: ((r + 2 * k) % 8, y, z))) for k in (1, 2, 3)]
    inv, first = block(core[None], own, other)
    inv_hi, inv_lo, far_hi, far_lo, cols = far(where, inv, first, nears)
    updated, panel_t = last(col, normal, wide, inv_hi, inv_lo, far_hi, far_lo, first, cols)
    return updated, panel_t.T


def solution(mesh):
    fine = Mesh(mesh.devices.reshape(4, 2, 4, 8), AXES)
    rows, cols = ("x", "core"), ("y", "z")
    return jax.shard_map(
        per_device,
        mesh=fine,
        in_specs=(P(rows, cols), P(None, AXES)),
        out_specs=(P(rows, cols), P(rows, cols)),
        check_vma=False,
    )
```

```python
import functools

import jax
import jax.numpy as jnp
from jax import lax
from jax.experimental import pallas as pl
from jax.experimental.pallas import tpu as pltpu
from jax.sharding import Mesh
from jax.sharding import PartitionSpec as P

PW = 512
NB = 16
T = 128
AXES = ("x", "core", "y", "z")
F32 = jnp.float32
BF16 = jnp.bfloat16
HI = lax.Precision.HIGHEST
VMEM = pltpu.VMEM


def nt(a, b, precision=None):
    return lax.dot_general(a, b, (((1,), (1,)), ((), ())), precision=precision, preferred_element_type=F32)


def nn(a, b, precision=None):
    return lax.dot_general(a, b, (((1,), (0,)), ((), ())), precision=precision, preferred_element_type=F32)


def tn(a, b):
    return lax.dot_general(a, b, (((0,), (0,)), ((), ())), preferred_element_type=F32)


def split(x):
    high = x.astype(BF16)
    return high, (x - high.astype(F32)).astype(BF16)


def prep_kernel(cols_ref, rows_ref, jac_ref, wide_ref, corner_ref, near_ref):
    cols = cols_ref[...].T[:NB]
    high, low = split(cols)
    for q in range(4):
        wide_ref[q] = high[:, q * PW : (q + 1) * PW]
        wide_ref[4 + q] = low[:, q * PW : (q + 1) * PW]
        wide_ref[8 + q] = jac_ref[q * NB : (q + 1) * NB, :]
    corner = jnp.concatenate([cols[:8, :64], cols[8:, :64]], axis=1)
    first = corner.astype(BF16).astype(F32)
    second = (corner - first).astype(BF16).astype(F32)
    third = corner - first - second
    corner_ref[:, :T] = jnp.concatenate([first, second], axis=0).astype(BF16)
    corner_ref[:, T:] = jnp.concatenate([third, third], axis=0).astype(BF16)
    high, low = split(rows_ref[...])
    for i in range(4):
        near_ref[i, :, :PW] = high[i * NB : (i + 1) * NB]
        near_ref[i, :, PW:] = low[i * NB : (i + 1) * NB]


def prep(normal, jac_t):
    rows = normal.shape[0]
    return pl.pallas_call(
        prep_kernel,
        grid=(1,),
        in_specs=[
            pl.BlockSpec((rows, T), lambda i: (0, 0)),
            pl.BlockSpec((64, PW), lambda i: (0, 0)),
            pl.BlockSpec((64, PW), lambda i: (0, 0)),
        ],
        out_specs=[
            pl.BlockSpec((12, NB, PW), lambda i: (0, 0, 0)),
            pl.BlockSpec((NB, 2 * T), lambda i: (0, 0)),
            pl.BlockSpec((4, NB, 2 * PW), lambda i: (0, 0, 0)),
        ],
        out_shape=[
            jax.ShapeDtypeStruct((12, NB, PW), BF16),
            jax.ShapeDtypeStruct((NB, 2 * T), BF16),
            jax.ShapeDtypeStruct((4, NB, 2 * PW), BF16),
        ],
        compiler_params=pltpu.CompilerParams(vmem_limit_bytes=62 << 20),
    )(normal, normal, jac_t)


def factor_tile(tile):
    q = 8
    groups = T // q
    rows = [tile[q * i : q * (i + 1), :] for i in range(groups)]
    lane = lax.broadcasted_iota(jnp.int32, (q, T), 1)
    out = []
    spread = lambda v: jnp.broadcast_to(v, (q, T))
    for g in range(groups):
        base = g * q
        cols = {i: [spread(rows[i][:, base + l : base + l + 1]) for l in range(q)] for i in range(g, groups)}
        low = [[None] * q for _ in range(q)]
        r = [None] * q
        pivot = [[spread(cols[g][l][k : k + 1, :]) if k >= l else None for l in range(q)] for k in range(q)]
        inside = (lane >= base) & (lane < base + q)
        done = [
            jnp.where(inside, jnp.where(lane == base + l, 1.0, 0.0), spread(rows[g][l : l + 1, :])) for l in range(q)
        ]
        near = list(cols[g + 1]) if g + 1 < groups else None
        for j in range(q):
            r[j] = lax.rsqrt(pivot[j][j])
            done[j] = done[j] * r[j]
            for i in range(j + 1, q):
                low[i][j] = pivot[i][j] * r[j]
            for i in range(j + 1, q):
                for k in range(j + 1, i + 1):
                    pivot[i][k] = pivot[i][k] - low[i][j] * low[k][j]
                done[i] = done[i] - low[i][j] * done[j]
            if near:
                near[j] = near[j] * r[j]
                for k in range(j + 1, q):
                    near[k] = near[k] - low[k][j] * near[j]
        weight = list(done)
        for j in range(q - 1, -1, -1):
            weight[j] = weight[j] * r[j]
            for i in range(j):
                weight[i] = weight[i] - low[j][i] * weight[j]
        sub = lax.broadcasted_iota(jnp.int32, (q, T), 0)
        mine = done[0]
        for k in range(1, q):
            mine = jnp.where(sub >= k, done[k], mine)
        out.append(jnp.where(lane < base + q, mine, 0.0))
        for i in range(g + 1, groups):
            left, right = (near, done) if i == g + 1 else (cols[i], weight)
            acc = left[0] * right[0]
            for k in range(1, q):
                acc = acc + left[k] * right[k]
            rows[i] = jnp.where(inside, 0.0, rows[i]) - acc
    return jnp.concatenate(out, 0)


def factor(work, inv):
    inv[...] = jnp.zeros_like(inv)
    tiles = PW // T
    for b in range(tiles):
        lo, hi = b * T, (b + 1) * T
        here = factor_tile(work[lo:hi, lo:hi])
        inv[lo:hi, lo:hi] = here
        if b:
            inv[lo:hi, :lo] = nn(here, inv[lo:hi, :lo], HI)
        if b < tiles - 1:
            below = nt(work[hi:, lo:hi], here, HI)
            work[hi : hi + T, hi : hi + T] -= nt(below[:T], below[:T], HI)
            if b < tiles - 2:
                work[hi + T :, hi:] -= nt(below[T:], below, HI)
            inv[hi:, :hi] -= nn(below, inv[lo:hi, :hi], HI)


def place(refs, core, store):
    for x in range(4):
        for ref, r in ((refs[0], 2 * x + core), (refs[1], 2 * x + 1 - core)):
            for a in range(4):
                store(ref, x, a, r)


def tile_rows(a, r):
    return pl.ds(pl.multiple_of(a * T + r * NB, NB), NB)


def block_kernel(core_ref, own_ref, other_ref, inv_ref, first_ref, work, pieces):
    core = core_ref[0]

    def store(ref, x, a, r):
        upper, lower = ref[x, a, :, :PW], ref[x, a, :, PW : 2 * PW]
        first_ref[tile_rows(a, r), :] = jnp.concatenate([upper, lower], axis=0).astype(BF16)
        lanes = pl.ds(pl.multiple_of(r * T, T), T)
        for z in range(8):
            start = 2 * PW + z * T
            pieces[(a * 8 + z) * 8 : (a * 8 + z + 1) * 8, lanes] = ref[x, a, :, start : start + T]

    place((own_ref, other_ref), core, store)
    src = lax.broadcasted_iota(jnp.int32, (8 * T, PW), 0)
    dst = lax.broadcasted_iota(jnp.int32, (8 * T, PW), 1)
    to = (src // 16 % 4) * T + (src // T) * NB + src % NB
    high, rest = split(pieces[...])
    rest = pieces[...] - high.astype(F32)
    middle, low = split(rest)
    for half in range(2):
        move = jnp.where((to == dst) & (src // 64 % 2 == half), 1.0, 0.0).astype(BF16)
        part = nn(high, move) + nn(middle, move) + nn(low, move)
        work.reshape(32, 2, 8, PW)[:, half] = part.reshape(32, 8, PW)
    first = first_ref[...]
    work[...] += nt(first, first)
    factor(work, inv_ref)


def block(core, own, other):
    whole = pl.BlockSpec(memory_space=VMEM)
    return pl.pallas_call(
        block_kernel,
        in_specs=[pl.BlockSpec(memory_space=pltpu.SMEM), whole, whole],
        out_specs=[whole] * 2,
        out_shape=[jax.ShapeDtypeStruct((PW, PW), F32), jax.ShapeDtypeStruct((PW, PW), BF16)],
        scratch_shapes=[VMEM((PW, PW), F32), VMEM((256, 8 * T), F32)],
        compiler_params=pltpu.CompilerParams(vmem_limit_bytes=62 << 20),
    )(core, own, other)


def last_kernel(
    col_ref, normal, wide, first, inv, near, out, panel_out,
    normal_in, wide_in, first_in, inv_in, near_in, out_buf, gram, cols, save, sem, sem_const, sem_out,
):
    chunks = []
    for q in range(4):
        jac = pl.ds(8 * q, 8), pl.ds(8, 4)
        rows = pl.ds(q * PW, PW)
        chunks.append(
            [
                pltpu.make_async_copy(wide.at[jac], wide_in.at[jac], sem.at[q, 0]),
                pltpu.make_async_copy(wide.at[:, q], wide_in.at[:, q], sem.at[q, 1]),
                pltpu.make_async_copy(wide.at[:, 4 + q], wide_in.at[:, 4 + q], sem.at[q, 2]),
                pltpu.make_async_copy(normal.at[rows], normal_in.at[rows], sem.at[q, 3]),
            ]
        )
    const = [
        pltpu.make_async_copy(near, near_in, sem_const.at[0]),
        pltpu.make_async_copy(first, first_in, sem_const.at[1]),
        pltpu.make_async_copy(inv, inv_in, sem_const.at[2]),
    ]
    for copy in const + chunks[0]:
        copy.start()
    const[0].wait()
    for r in range(8):
        for a in range(4):
            at = slice(a * T + r * NB, a * T + (r + 1) * NB)
            cols[at, :] = near_in[r, a, :, :PW]
            gram[at, :] = near_in[r, a, :, PW : 2 * PW].astype(F32) + near_in[r, a, :, 2 * PW :].astype(F32)
    const[1].wait()
    right, rest = split(gram[...] + nt(first_in[...], cols[...]))
    const[2].wait()
    inv_hi, inv_lo = split(inv_in[...])
    far_hi, far_lo = split(nn(inv_hi, right) + (nn(inv_lo, right) + nn(inv_hi, rest)))
    moves_out = []
    at_panel = pl.ds(pl.multiple_of(col_ref[0] * NB, NB), NB)
    for q in range(4):
        for copy in chunks[q]:
            copy.wait()
        if q < 3:
            for copy in chunks[q + 1]:
                copy.start()
        rows = slice(q * PW, (q + 1) * PW)
        jac_rows = wide_in[8 * q : 8 * q + 8, 8:12].reshape(PW, PW)
        panel_in = wide_in[:, q].reshape(PW, PW).astype(F32) + wide_in[:, 4 + q].reshape(PW, PW).astype(F32)
        high, low = split(panel_in + nt(first_in[...], jac_rows))
        panel = nn(inv_hi, high) + (nn(inv_lo, high) + nn(inv_hi, low))
        save[...] = panel
        panel_out[:, rows] = save[at_panel, :]
        high, low = split(panel)
        drop = tn(high, far_hi) + (tn(low, far_hi) + tn(high, far_lo))
        out_buf[rows, :] = normal_in[rows, :] + nt(jac_rows, cols[...]) - drop
        moves_out.append(
            pltpu.make_async_copy(out_buf.at[pl.ds(q * PW, PW)], out.at[pl.ds(q * PW, PW)], sem_out.at[q])
        )
        moves_out[q].start()
    for copy in moves_out:
        copy.wait()


def last(col, normal, wide, first, inv, near):
    rows = normal.shape[0]
    there = pl.BlockSpec(memory_space=pl.ANY)
    return pl.pallas_call(
        last_kernel,
        in_specs=[pl.BlockSpec(memory_space=pltpu.SMEM)] + [there] * 5,
        out_specs=[there, pl.BlockSpec(memory_space=VMEM)],
        out_shape=[
            jax.ShapeDtypeStruct((rows, PW), F32),
            jax.ShapeDtypeStruct((NB, rows), F32),
        ],
        scratch_shapes=[
            VMEM((rows, PW), F32),
            VMEM((32, 12, NB, PW), BF16),
            VMEM((PW, PW), BF16),
            VMEM((PW, PW), F32),
            VMEM((8, 4, NB, 3 * PW), BF16),
            VMEM((rows, PW), F32),
            VMEM((PW, PW), F32),
            VMEM((PW, PW), BF16),
            VMEM((PW, PW), F32),
            pltpu.SemaphoreType.DMA((4, 4)),
            pltpu.SemaphoreType.DMA((3,)),
            pltpu.SemaphoreType.DMA((4,)),
        ],
        compiler_params=pltpu.CompilerParams(vmem_limit_bytes=62 << 20),
    )(col, normal, wide, first, inv, near)


def position(r, y, z):
    return (r * 4 + y) * 8 + z


def spread_over(value, axis, count):
    return lax.all_to_all(jnp.broadcast_to(value[None], (count,) + value.shape), axis, 0, 0, tiled=True)


def moves(to):
    return [(position(r, y, z), position(*to(r, y, z))) for r in range(8) for y in range(4) for z in range(8)]


def per_device(normal, jacobian):
    core = lax.axis_index("core").astype(jnp.int32)[None]
    col = (lax.axis_index("y") * 8 + lax.axis_index("z")).astype(jnp.int32)[None]
    jac_t = jacobian.T
    wide, corner, near = prep(normal, jac_t)
    wide = lax.all_gather(wide, ("y", "z"), axis=0, tiled=False)
    tiles = lax.all_to_all(jac_t.reshape(4, NB, PW), "y", 0, 0, tiled=True)
    swapped = lax.ppermute(tiles, AXES, moves(lambda r, y, z: (z, y, r)))
    near = jnp.concatenate([swapped, near], axis=2)
    got = spread_over(jnp.concatenate([tiles[0], corner], axis=1), "z", 8)
    head = got[0, :, :PW].astype(F32)
    parts = got[:, :, PW:].astype(F32)
    parts = parts[:, :8, :T] + parts[:, 8:, :T] + parts[:, :8, T:]
    sent = jnp.concatenate([head[:8], head[8:]] + [parts[z] for z in range(8)], axis=1)
    got = spread_over(sent, "y", 4)
    own = spread_over(got, "x", 4)
    other = lax.ppermute(own, AXES, moves(lambda r, y, z: (r ^ 1, y, z)))
    near = spread_over(near, ("x", "core"), 8)
    inv, first = block(core, own, other)
    updated, panel_t = last(col, normal, wide, first, inv, near)
    return updated, panel_t.T


def solution(mesh):
    fine = Mesh(mesh.devices.reshape(4, 2, 4, 8), AXES)
    rows, cols = ("x", "core"), ("y", "z")
    return jax.shard_map(
        per_device,
        mesh=fine,
        in_specs=(P(rows, cols), P(None, AXES)),
        out_specs=(P(rows, cols), P(rows, cols)),
        check_vma=False,
    )
```

```python
import functools

import jax
import jax.numpy as jnp
from jax import lax
from jax.experimental import pallas as pl
from jax.experimental.pallas import tpu as pltpu
from jax.sharding import Mesh
from jax.sharding import PartitionSpec as P

PW = 512
NB = 16
T = 128
AXES = ("x", "core", "y", "z")
F32 = jnp.float32
BF16 = jnp.bfloat16
HI = lax.Precision.HIGHEST
VMEM = pltpu.VMEM


def nt(a, b, precision=None):
    return lax.dot_general(a, b, (((1,), (1,)), ((), ())), precision=precision, preferred_element_type=F32)


def nn(a, b, precision=None):
    return lax.dot_general(a, b, (((1,), (0,)), ((), ())), precision=precision, preferred_element_type=F32)


def tn(a, b):
    return lax.dot_general(a, b, (((0,), (0,)), ((), ())), preferred_element_type=F32)


def split(x):
    high = x.astype(BF16)
    return high, (x - high.astype(F32)).astype(BF16)


def prep_kernel(cols_ref, rows_ref, jac_ref, wide_ref, corner_ref, near_ref):
    cols = cols_ref[...].T[:NB]
    high, low = split(cols)
    for q in range(4):
        wide_ref[q] = high[:, q * PW : (q + 1) * PW]
        wide_ref[4 + q] = low[:, q * PW : (q + 1) * PW]
        wide_ref[8 + q] = jac_ref[q * NB : (q + 1) * NB, :]
    corner = jnp.concatenate([cols[:8, :64], cols[8:, :64]], axis=1)
    first = corner.astype(BF16).astype(F32)
    second = (corner - first).astype(BF16).astype(F32)
    third = corner - first - second
    corner_ref[:, :T] = jnp.concatenate([first, second], axis=0).astype(BF16)
    corner_ref[:, T:] = jnp.concatenate([third, third], axis=0).astype(BF16)
    high, low = split(rows_ref[...])
    for i in range(4):
        near_ref[i, :, :PW] = high[i * NB : (i + 1) * NB]
        near_ref[i, :, PW:] = low[i * NB : (i + 1) * NB]


def prep(normal, jac_t):
    rows = normal.shape[0]
    return pl.pallas_call(
        prep_kernel,
        grid=(1,),
        in_specs=[
            pl.BlockSpec((rows, T), lambda i: (0, 0)),
            pl.BlockSpec((64, PW), lambda i: (0, 0)),
            pl.BlockSpec((64, PW), lambda i: (0, 0)),
        ],
        out_specs=[
            pl.BlockSpec((12, NB, PW), lambda i: (0, 0, 0)),
            pl.BlockSpec((NB, 2 * T), lambda i: (0, 0)),
            pl.BlockSpec((4, NB, 2 * PW), lambda i: (0, 0, 0)),
        ],
        out_shape=[
            jax.ShapeDtypeStruct((12, NB, PW), BF16),
            jax.ShapeDtypeStruct((NB, 2 * T), BF16),
            jax.ShapeDtypeStruct((4, NB, 2 * PW), BF16),
        ],
        compiler_params=pltpu.CompilerParams(vmem_limit_bytes=62 << 20),
    )(normal, normal, jac_t)


def factor_tile(tile):
    q = 8
    groups = T // q
    rows = [tile[q * i : q * (i + 1), :] for i in range(groups)]
    lane = lax.broadcasted_iota(jnp.int32, (q, T), 1)
    out = []
    spread = lambda v: jnp.broadcast_to(v, (q, T))
    for g in range(groups):
        base = g * q
        cols = {i: [spread(rows[i][:, base + l : base + l + 1]) for l in range(q)] for i in range(g, groups)}
        low = [[None] * q for _ in range(q)]
        r = [None] * q
        pivot = [[spread(cols[g][l][k : k + 1, :]) if k >= l else None for l in range(q)] for k in range(q)]
        inside = (lane >= base) & (lane < base + q)
        done = [
            jnp.where(inside, jnp.where(lane == base + l, 1.0, 0.0), spread(rows[g][l : l + 1, :])) for l in range(q)
        ]
        near = list(cols[g + 1]) if g + 1 < groups else None
        for j in range(q):
            r[j] = lax.rsqrt(pivot[j][j])
            done[j] = done[j] * r[j]
            for i in range(j + 1, q):
                low[i][j] = pivot[i][j] * r[j]
            for i in range(j + 1, q):
                for k in range(j + 1, i + 1):
                    pivot[i][k] = pivot[i][k] - low[i][j] * low[k][j]
                done[i] = done[i] - low[i][j] * done[j]
            if near:
                near[j] = near[j] * r[j]
                for k in range(j + 1, q):
                    near[k] = near[k] - low[k][j] * near[j]
        weight = list(done)
        for j in range(q - 1, -1, -1):
            weight[j] = weight[j] * r[j]
            for i in range(j):
                weight[i] = weight[i] - low[j][i] * weight[j]
        sub = lax.broadcasted_iota(jnp.int32, (q, T), 0)
        mine = done[0]
        for k in range(1, q):
            mine = jnp.where(sub >= k, done[k], mine)
        out.append(jnp.where(lane < base + q, mine, 0.0))
        for i in range(g + 1, groups):
            left, right = (near, done) if i == g + 1 else (cols[i], weight)
            acc = left[0] * right[0]
            for k in range(1, q):
                acc = acc + left[k] * right[k]
            rows[i] = jnp.where(inside, 0.0, rows[i]) - acc
    return jnp.concatenate(out, 0)


def factor(work, inv):
    inv[...] = jnp.zeros_like(inv)
    tiles = PW // T
    for b in range(tiles):
        lo, hi = b * T, (b + 1) * T
        here = factor_tile(work[lo:hi, lo:hi])
        inv[lo:hi, lo:hi] = here
        if b:
            inv[lo:hi, :lo] = nn(here, inv[lo:hi, :lo], HI)
        if b < tiles - 1:
            below = nt(work[hi:, lo:hi], here, HI)
            work[hi : hi + T, hi : hi + T] -= nt(below[:T], below[:T], HI)
            if b < tiles - 2:
                work[hi + T :, hi:] -= nt(below[T:], below, HI)
            inv[hi:, :hi] -= nn(below, inv[lo:hi, :hi], HI)


def place(refs, core, store):
    for x in range(4):
        for ref, r in ((refs[0], 2 * x + core), (refs[1], 2 * x + 1 - core)):
            for a in range(4):
                store(ref, x, a, r)


def tile_rows(a, r):
    return pl.ds(pl.multiple_of(a * T + r * NB, NB), NB)


def block_kernel(core_ref, own_ref, other_ref, inv_ref, first_ref, work, pieces):
    core = core_ref[0]

    def store(ref, x, a, r):
        upper, lower = ref[x, a, :, :PW], ref[x, a, :, PW : 2 * PW]
        first_ref[tile_rows(a, r), :] = jnp.concatenate([upper, lower], axis=0).astype(BF16)
        lanes = pl.ds(pl.multiple_of(r * T, T), T)
        for z in range(8):
            start = 2 * PW + z * T
            pieces[(a * 8 + z) * 8 : (a * 8 + z + 1) * 8, lanes] = ref[x, a, :, start : start + T]

    place((own_ref, other_ref), core, store)
    src = lax.broadcasted_iota(jnp.int32, (8 * T, PW), 0)
    dst = lax.broadcasted_iota(jnp.int32, (8 * T, PW), 1)
    to = (src // 16 % 4) * T + (src // T) * NB + src % NB
    high, rest = split(pieces[...])
    rest = pieces[...] - high.astype(F32)
    middle, low = split(rest)
    for half in range(2):
        move = jnp.where((to == dst) & (src // 64 % 2 == half), 1.0, 0.0).astype(BF16)
        part = nn(high, move) + nn(middle, move) + nn(low, move)
        work.reshape(32, 2, 8, PW)[:, half] = part.reshape(32, 8, PW)
    first = first_ref[...]
    work[...] += nt(first, first)
    factor(work, inv_ref)


def block(core, own, other):
    whole = pl.BlockSpec(memory_space=VMEM)
    return pl.pallas_call(
        block_kernel,
        in_specs=[pl.BlockSpec(memory_space=pltpu.SMEM), whole, whole],
        out_specs=[whole] * 2,
        out_shape=[jax.ShapeDtypeStruct((PW, PW), F32), jax.ShapeDtypeStruct((PW, PW), BF16)],
        scratch_shapes=[VMEM((PW, PW), F32), VMEM((256, 8 * T), F32)],
        compiler_params=pltpu.CompilerParams(vmem_limit_bytes=62 << 20),
    )(core, own, other)


def split3(x):
    high, rest = x.astype(BF16), x - x.astype(BF16).astype(F32)
    middle, low = split(rest)
    return high, middle, low


def far_kernel(col_ref, inv_ref, first_ref, near, w_hi, w_lo, v_hi, v_lo, own_rows, own_jac, cols, gram):
    for r in range(8):
        for a in range(4):
            at = slice(a * T + r * NB, a * T + (r + 1) * NB)
            cols[at, :] = near[r, a, :, :PW]
            gram[at, :] = near[r, a, :, PW : 2 * PW].astype(F32) + near[r, a, :, 2 * PW :].astype(F32)
    first = first_ref[...]
    inv = inv_ref[...]
    panel = nn(inv, gram[...] + nt(first, cols[...]), HI)
    weight = nn(inv.T, panel, HI)
    high, middle, low = split3(weight)
    w_hi[...] = high
    w_lo[...] = middle
    change = tn(high, first) + (tn(middle, first) + tn(low, first))
    high, low = split(cols[...].astype(F32) - change)
    v_hi[...] = high
    v_lo[...] = low
    mine = inv_ref[pl.ds(pl.multiple_of(col_ref[0] * NB, NB), NB), :]
    high, middle, low = split3(mine)
    own_rows[:NB, :] = high
    own_rows[NB:, :] = middle
    high, low = split(nn(high, first) + (nn(middle, first) + nn(low, first)))
    own_jac[:NB, :] = high
    own_jac[NB:, :] = low


def far(col, inv, first, near):
    whole = pl.BlockSpec(memory_space=VMEM)
    return pl.pallas_call(
        far_kernel,
        in_specs=[pl.BlockSpec(memory_space=pltpu.SMEM)] + [whole] * 3,
        out_specs=[whole] * 6,
        out_shape=[jax.ShapeDtypeStruct((PW, PW), BF16)] * 4 + [jax.ShapeDtypeStruct((2 * NB, PW), BF16)] * 2,
        scratch_shapes=[VMEM((PW, PW), BF16), VMEM((PW, PW), F32)],
        compiler_params=pltpu.CompilerParams(vmem_limit_bytes=62 << 20),
    )(col, inv, first, near)


def last_kernel(
    normal, wide, w_hi, w_lo, v_hi, v_lo, own_rows, own_jac, out, panel_out,
    normal_in, wide_in, w_hi_in, w_lo_in, v_hi_in, v_lo_in, out_buf, sem, sem_const, sem_out,
):
    chunks = []
    for q in range(4):
        jac = pl.ds(8 * q, 8), pl.ds(8, 4)
        rows = pl.ds(q * PW, PW)
        chunks.append(
            [
                pltpu.make_async_copy(wide.at[jac], wide_in.at[jac], sem.at[q, 0]),
                pltpu.make_async_copy(wide.at[:, q], wide_in.at[:, q], sem.at[q, 1]),
                pltpu.make_async_copy(wide.at[:, 4 + q], wide_in.at[:, 4 + q], sem.at[q, 2]),
                pltpu.make_async_copy(normal.at[rows], normal_in.at[rows], sem.at[q, 3]),
            ]
        )
    const = [
        pltpu.make_async_copy(src, dst, sem_const.at[k])
        for k, (src, dst) in enumerate(((v_hi, v_hi_in), (v_lo, v_lo_in), (w_hi, w_hi_in), (w_lo, w_lo_in)))
    ]
    for copy in (chunks[0][0], const[0], const[1], chunks[0][1], const[2], const[3], chunks[0][2], chunks[0][3]):
        copy.start()
    moves_out = []
    for q in range(4):
        rows = slice(q * PW, (q + 1) * PW)
        chunks[q][0].wait()
        if q == 0:
            const[0].wait()
            const[1].wait()
        jac_rows = wide_in[8 * q : 8 * q + 8, 8:12].reshape(PW, PW)
        sums = nt(jac_rows, v_hi_in[...]) + nt(jac_rows, v_lo_in[...])
        mine = nt(own_jac[...], jac_rows)
        if q == 0:
            const[2].wait()
            const[3].wait()
        for copy in chunks[q][1:]:
            copy.wait()
        if q < 3:
            for copy in chunks[q + 1]:
                copy.start()
        high = wide_in[:, q].reshape(PW, PW)
        low = wide_in[:, 4 + q].reshape(PW, PW)
        drop = tn(high, w_hi_in[...]) + (tn(low, w_hi_in[...]) + tn(high, w_lo_in[...]))
        out_buf[rows, :] = normal_in[rows, :] + (sums - drop)
        moves_out.append(
            pltpu.make_async_copy(out_buf.at[pl.ds(q * PW, PW)], out.at[pl.ds(q * PW, PW)], sem_out.at[q])
        )
        moves_out[q].start()
        mine = mine + nn(own_rows[...], high)
        panel_out[:, rows] = mine[:NB] + mine[NB:] + nn(own_rows[:NB], low)
    for copy in moves_out:
        copy.wait()


def last(normal, wide, w_hi, w_lo, v_hi, v_lo, own_rows, own_jac):
    rows = normal.shape[0]
    there = pl.BlockSpec(memory_space=pl.ANY)
    whole = pl.BlockSpec(memory_space=VMEM)
    return pl.pallas_call(
        last_kernel,
        in_specs=[there] * 6 + [whole] * 2,
        out_specs=[there, whole],
        out_shape=[
            jax.ShapeDtypeStruct((rows, PW), F32),
            jax.ShapeDtypeStruct((NB, rows), F32),
        ],
        scratch_shapes=[VMEM((rows, PW), F32), VMEM((32, 12, NB, PW), BF16)]
        + [VMEM((PW, PW), BF16)] * 4
        + [
            VMEM((rows, PW), F32),
            pltpu.SemaphoreType.DMA((4, 4)),
            pltpu.SemaphoreType.DMA((4,)),
            pltpu.SemaphoreType.DMA((4,)),
        ],
        compiler_params=pltpu.CompilerParams(vmem_limit_bytes=62 << 20),
    )(normal, wide, w_hi, w_lo, v_hi, v_lo, own_rows, own_jac)


def position(r, y, z):
    return (r * 4 + y) * 8 + z


def spread_over(value, axis, count):
    return lax.all_to_all(jnp.broadcast_to(value[None], (count,) + value.shape), axis, 0, 0, tiled=True)


def moves(to):
    return [(position(r, y, z), position(*to(r, y, z))) for r in range(8) for y in range(4) for z in range(8)]


def per_device(normal, jacobian):
    core = lax.axis_index("core").astype(jnp.int32)[None]
    col = (lax.axis_index("y") * 8 + lax.axis_index("z")).astype(jnp.int32)[None]
    jac_t = jacobian.T
    wide, corner, near = prep(normal, jac_t)
    wide = lax.all_gather(wide, ("y", "z"), axis=0, tiled=False)
    tiles = lax.all_to_all(jac_t.reshape(4, NB, PW), "y", 0, 0, tiled=True)
    swapped = lax.ppermute(tiles, AXES, moves(lambda r, y, z: (z, y, r)))
    near = jnp.concatenate([swapped, near], axis=2)
    got = spread_over(jnp.concatenate([tiles[0], corner], axis=1), "z", 8)
    head = got[0, :, :PW].astype(F32)
    parts = got[:, :, PW:].astype(F32)
    parts = parts[:, :8, :T] + parts[:, 8:, :T] + parts[:, :8, T:]
    sent = jnp.concatenate([head[:8], head[8:]] + [parts[z] for z in range(8)], axis=1)
    own = spread_over(sent, ("x", "y"), 16).reshape(4, 4, 8, 4 * PW)
    other = lax.ppermute(own, AXES, moves(lambda r, y, z: (r ^ 1, y, z)))
    near = spread_over(near, ("x", "core"), 8)
    inv, first = block(core, own, other)
    updated, panel_t = last(normal, wide, *far(col, inv, first, near))
    return updated, panel_t.T


def solution(mesh):
    fine = Mesh(mesh.devices.reshape(4, 2, 4, 8), AXES)
    rows, cols = ("x", "core"), ("y", "z")
    return jax.shard_map(
        per_device,
        mesh=fine,
        in_specs=(P(rows, cols), P(None, AXES)),
        out_specs=(P(rows, cols), P(rows, cols)),
        check_vma=False,
    )
```

```python
import functools

import jax
import jax.numpy as jnp
from jax import lax
from jax.experimental import pallas as pl
from jax.experimental.pallas import tpu as pltpu
from jax.sharding import Mesh
from jax.sharding import PartitionSpec as P

PW = 512
NB = 16
T = 128
AXES = ("x", "core", "y", "z")
F32 = jnp.float32
BF16 = jnp.bfloat16
HI = lax.Precision.HIGHEST
VMEM = pltpu.VMEM


def nt(a, b, precision=None):
    return lax.dot_general(a, b, (((1,), (1,)), ((), ())), precision=precision, preferred_element_type=F32)


def nn(a, b, precision=None):
    return lax.dot_general(a, b, (((1,), (0,)), ((), ())), precision=precision, preferred_element_type=F32)


def tn(a, b):
    return lax.dot_general(a, b, (((0,), (0,)), ((), ())), preferred_element_type=F32)


def in_vmem(x):
    return pltpu.with_memory_space_constraint(x, pltpu.VMEM)


def in_hbm(x):
    return pltpu.with_memory_space_constraint(x, pltpu.HBM)


def split(x):
    high = x.astype(BF16)
    return high, (x - high.astype(F32)).astype(BF16)


def prep_kernel(cols_ref, rows_ref, jac_ref, wide_ref, corner_ref, near_ref):
    cols = cols_ref[...].T[:NB]
    high, low = split(cols)
    for q in range(4):
        wide_ref[q] = high[:, q * PW : (q + 1) * PW]
        wide_ref[4 + q] = low[:, q * PW : (q + 1) * PW]
        wide_ref[8 + q] = jac_ref[q * NB : (q + 1) * NB, :]
    corner = jnp.concatenate([cols[:8, :64], cols[8:, :64]], axis=1)
    first = corner.astype(BF16).astype(F32)
    second = (corner - first).astype(BF16).astype(F32)
    third = corner - first - second
    corner_ref[:, :T] = jnp.concatenate([first, second], axis=0).astype(BF16)
    corner_ref[:, T:] = jnp.concatenate([third, third], axis=0).astype(BF16)
    high, low = split(rows_ref[...])
    for i in range(4):
        near_ref[i, :, :PW] = high[i * NB : (i + 1) * NB]
        near_ref[i, :, PW:] = low[i * NB : (i + 1) * NB]


def prep(normal, jac_t):
    rows = normal.shape[0]
    return pl.pallas_call(
        prep_kernel,
        grid=(1,),
        in_specs=[
            pl.BlockSpec((rows, T), lambda i: (0, 0)),
            pl.BlockSpec((64, PW), lambda i: (0, 0)),
            pl.BlockSpec((64, PW), lambda i: (0, 0)),
        ],
        out_specs=[
            pl.BlockSpec((12, NB, PW), lambda i: (0, 0, 0)),
            pl.BlockSpec((NB, 2 * T), lambda i: (0, 0)),
            pl.BlockSpec((4, NB, 2 * PW), lambda i: (0, 0, 0)),
        ],
        out_shape=[
            jax.ShapeDtypeStruct((12, NB, PW), BF16),
            jax.ShapeDtypeStruct((NB, 2 * T), BF16),
            jax.ShapeDtypeStruct((4, NB, 2 * PW), BF16),
        ],
        compiler_params=pltpu.CompilerParams(vmem_limit_bytes=62 << 20),
    )(normal, normal, jac_t)


def factor_tile(tile):
    q = 8
    groups = T // q
    rows = [tile[q * i : q * (i + 1), :] for i in range(groups)]
    lane = lax.broadcasted_iota(jnp.int32, (q, T), 1)
    out = []
    spread = lambda v: jnp.broadcast_to(v, (q, T))
    for g in range(groups):
        base = g * q
        cols = {i: [spread(rows[i][:, base + l : base + l + 1]) for l in range(q)] for i in range(g, groups)}
        low = [[None] * q for _ in range(q)]
        r = [None] * q
        pivot = [[spread(cols[g][l][k : k + 1, :]) if k >= l else None for l in range(q)] for k in range(q)]
        inside = (lane >= base) & (lane < base + q)
        done = [
            jnp.where(inside, jnp.where(lane == base + l, 1.0, 0.0), spread(rows[g][l : l + 1, :])) for l in range(q)
        ]
        near = list(cols[g + 1]) if g + 1 < groups else None
        for j in range(q):
            r[j] = lax.rsqrt(pivot[j][j])
            done[j] = done[j] * r[j]
            for i in range(j + 1, q):
                low[i][j] = pivot[i][j] * r[j]
            for i in range(j + 1, q):
                for k in range(j + 1, i + 1):
                    pivot[i][k] = pivot[i][k] - low[i][j] * low[k][j]
                done[i] = done[i] - low[i][j] * done[j]
            if near:
                near[j] = near[j] * r[j]
                for k in range(j + 1, q):
                    near[k] = near[k] - low[k][j] * near[j]
        weight = list(done)
        for j in range(q - 1, -1, -1):
            weight[j] = weight[j] * r[j]
            for i in range(j):
                weight[i] = weight[i] - low[j][i] * weight[j]
        sub = lax.broadcasted_iota(jnp.int32, (q, T), 0)
        mine = done[0]
        for k in range(1, q):
            mine = jnp.where(sub >= k, done[k], mine)
        out.append(jnp.where(lane < base + q, mine, 0.0))
        for i in range(g + 1, groups):
            left, right = (near, done) if i == g + 1 else (cols[i], weight)
            acc = left[0] * right[0]
            for k in range(1, q):
                acc = acc + left[k] * right[k]
            rows[i] = jnp.where(inside, 0.0, rows[i]) - acc
    return jnp.concatenate(out, 0)


def factor(work, inv):
    inv[...] = jnp.zeros_like(inv)
    tiles = PW // T
    for b in range(tiles):
        lo, hi = b * T, (b + 1) * T
        here = factor_tile(work[lo:hi, lo:hi])
        inv[lo:hi, lo:hi] = here
        if b:
            inv[lo:hi, :lo] = nn(here, inv[lo:hi, :lo], HI)
        if b < tiles - 1:
            below = nt(work[hi:, lo:hi], here, HI)
            work[hi : hi + T, hi : hi + T] -= nt(below[:T], below[:T], HI)
            if b < tiles - 2:
                work[hi + T :, hi:] -= nt(below[T:], below, HI)
            inv[hi:, :hi] -= nn(below, inv[lo:hi, :hi], HI)


def place(refs, core, store):
    for x in range(4):
        for ref, r in ((refs[0], 2 * x + core), (refs[1], 2 * x + 1 - core)):
            for a in range(4):
                store(ref, x, a, r)


def tile_rows(a, r):
    return pl.ds(pl.multiple_of(a * T + r * NB, NB), NB)


def block_kernel(core_ref, own_ref, other_ref, inv_ref, first_ref, work, pieces):
    core = core_ref[0]

    def store(ref, x, a, r):
        upper, lower = ref[x, a, :, :PW], ref[x, a, :, PW : 2 * PW]
        first_ref[tile_rows(a, r), :] = jnp.concatenate([upper, lower], axis=0).astype(BF16)
        lanes = pl.ds(pl.multiple_of(r * T, T), T)
        for z in range(8):
            start = 2 * PW + z * T
            pieces[(a * 8 + z) * 8 : (a * 8 + z + 1) * 8, lanes] = ref[x, a, :, start : start + T]

    place((own_ref, other_ref), core, store)
    src = lax.broadcasted_iota(jnp.int32, (8 * T, PW), 0)
    dst = lax.broadcasted_iota(jnp.int32, (8 * T, PW), 1)
    to = (src // 16 % 4) * T + (src // T) * NB + src % NB
    high, rest = split(pieces[...])
    rest = pieces[...] - high.astype(F32)
    middle, low = split(rest)
    for half in range(2):
        move = jnp.where((to == dst) & (src // 64 % 2 == half), 1.0, 0.0).astype(BF16)
        part = nn(high, move) + nn(middle, move) + nn(low, move)
        work.reshape(32, 2, 8, PW)[:, half] = part.reshape(32, 8, PW)
    first = first_ref[...]
    work[...] += nt(first, first)
    factor(work, inv_ref)


def block(core, own, other):
    whole = pl.BlockSpec(memory_space=VMEM)
    return pl.pallas_call(
        block_kernel,
        in_specs=[pl.BlockSpec(memory_space=pltpu.SMEM), whole, whole],
        out_specs=[whole] * 2,
        out_shape=[VMEM((PW, PW), F32), jax.ShapeDtypeStruct((PW, PW), BF16)],
        scratch_shapes=[VMEM((PW, PW), F32), VMEM((256, 8 * T), F32)],
        compiler_params=pltpu.CompilerParams(vmem_limit_bytes=48 << 20),
    )(core, own, other)


def split3(x):
    high, rest = x.astype(BF16), x - x.astype(BF16).astype(F32)
    middle, low = split(rest)
    return high, middle, low


def far_kernel(col_ref, inv_ref, first_ref, near, w_hi, w_lo, v_hi, v_lo, own_rows, own_jac, cols, gram):
    for r in range(8):
        for a in range(4):
            at = slice(a * T + r * NB, a * T + (r + 1) * NB)
            cols[at, :] = near[r, a, :, :PW]
            gram[at, :] = near[r, a, :, PW : 2 * PW].astype(F32) + near[r, a, :, 2 * PW :].astype(F32)
    first = first_ref[...]
    inv = inv_ref[...]
    panel = nn(inv, gram[...] + nt(first, cols[...]), HI)
    weight = nn(inv.T, panel, HI)
    high, middle, low = split3(weight)
    w_hi[...] = high
    w_lo[...] = middle
    change = tn(high, first) + (tn(middle, first) + tn(low, first))
    high, low = split(cols[...].astype(F32) - change)
    v_hi[...] = high
    v_lo[...] = low
    mine = inv_ref[pl.ds(pl.multiple_of(col_ref[0] * NB, NB), NB), :]
    high, middle, low = split3(mine)
    own_rows[:NB, :] = high
    own_rows[NB:, :] = middle
    high, low = split(nn(high, first) + (nn(middle, first) + nn(low, first)))
    own_jac[:NB, :] = high
    own_jac[NB:, :] = low


def far(col, inv, first, near):
    whole = pl.BlockSpec(memory_space=VMEM)
    return pl.pallas_call(
        far_kernel,
        in_specs=[pl.BlockSpec(memory_space=pltpu.SMEM)] + [whole] * 3,
        out_specs=[whole] * 6,
        out_shape=[VMEM((PW, PW), BF16), jax.ShapeDtypeStruct((PW, PW), BF16)]
        + [VMEM((PW, PW), BF16)] * 2
        + [VMEM((2 * NB, PW), BF16)] * 2,
        scratch_shapes=[VMEM((PW, PW), BF16), VMEM((PW, PW), F32)],
        compiler_params=pltpu.CompilerParams(vmem_limit_bytes=48 << 20),
    )(col, in_vmem(inv), first, near)


def last_kernel(
    normal, wide, w_lo, w_hi, v_hi, v_lo, own_rows, own_jac, out, panel_out,
    wide_in, normal_in, w_lo_in, out_buf, sem, sem_w, sem_out,
):
    chunks = []
    for q in range(4):
        jac = pl.ds(8 * q, 8), pl.ds(8, 4)
        rows = pl.ds(q * PW, PW)
        chunks.append(
            [
                pltpu.make_async_copy(wide.at[jac], wide_in.at[jac], sem.at[q, 0]),
                pltpu.make_async_copy(wide.at[:, q], wide_in.at[:, q], sem.at[q, 1]),
                pltpu.make_async_copy(wide.at[:, 4 + q], wide_in.at[:, 4 + q], sem.at[q, 2]),
                pltpu.make_async_copy(normal.at[rows], normal_in.at[rows], sem.at[q, 3]),
            ]
        )
    copy_w = pltpu.make_async_copy(w_lo, w_lo_in, sem_w)
    for copy in chunks[0][:3] + [copy_w] + chunks[0][3:]:
        copy.start()
    moves_out = []
    for q in range(4):
        rows = slice(q * PW, (q + 1) * PW)
        chunks[q][0].wait()
        jac_rows = wide_in[8 * q : 8 * q + 8, 8:12].reshape(PW, PW)
        sums = nt(jac_rows, v_hi[...]) + nt(jac_rows, v_lo[...])
        mine = nt(own_jac[...], jac_rows)
        for copy in chunks[q][1:] + [copy_w] * (q == 0):
            copy.wait()
        if q < 3:
            for copy in chunks[q + 1]:
                copy.start()
        high = wide_in[:, q].reshape(PW, PW)
        low = wide_in[:, 4 + q].reshape(PW, PW)
        drop = tn(high, w_hi[...]) + (tn(low, w_hi[...]) + tn(high, w_lo_in[...]))
        out_buf[rows, :] = normal_in[rows, :] + (sums - drop)
        moves_out.append(
            pltpu.make_async_copy(out_buf.at[pl.ds(q * PW, PW)], out.at[pl.ds(q * PW, PW)], sem_out.at[q])
        )
        moves_out[q].start()
        mine = mine + nn(own_rows[...], high)
        panel_out[:, rows] = mine[:NB] + mine[NB:] + nn(own_rows[:NB], low)
    for copy in moves_out:
        copy.wait()


def last(normal, wide, w_hi, w_lo, *parts):
    rows = normal.shape[0]
    there = pl.BlockSpec(memory_space=pl.ANY)
    whole = pl.BlockSpec(memory_space=VMEM)
    return pl.pallas_call(
        last_kernel,
        in_specs=[there] * 3 + [whole] * 5,
        out_specs=[there, whole],
        out_shape=[
            jax.ShapeDtypeStruct((rows, PW), F32),
            jax.ShapeDtypeStruct((NB, rows), F32),
        ],
        scratch_shapes=[
            VMEM((32, 12, NB, PW), BF16),
            VMEM((rows, PW), F32),
            VMEM((PW, PW), BF16),
            VMEM((rows, PW), F32),
            pltpu.SemaphoreType.DMA((4, 4)),
            pltpu.SemaphoreType.DMA,
            pltpu.SemaphoreType.DMA((4,)),
        ],
        compiler_params=pltpu.CompilerParams(vmem_limit_bytes=48 << 20),
    )(in_hbm(normal), in_hbm(wide), in_hbm(w_lo), in_vmem(w_hi), *(in_vmem(part) for part in parts))


def position(r, y, z):
    return (r * 4 + y) * 8 + z


def spread_over(value, axis, count):
    return lax.all_to_all(jnp.broadcast_to(value[None], (count,) + value.shape), axis, 0, 0, tiled=True)


def moves(to):
    return [(position(r, y, z), position(*to(r, y, z))) for r in range(8) for y in range(4) for z in range(8)]


def per_device(normal, jacobian):
    core = lax.axis_index("core").astype(jnp.int32)[None]
    col = (lax.axis_index("y") * 8 + lax.axis_index("z")).astype(jnp.int32)[None]
    jac_t = jacobian.T
    wide, corner, near = prep(normal, jac_t)
    wide = lax.all_gather(wide, ("y", "z"), axis=0, tiled=False)
    tiles = lax.all_to_all(jac_t.reshape(4, NB, PW), "y", 0, 0, tiled=True)
    swapped = lax.ppermute(tiles, AXES, moves(lambda r, y, z: (z, y, r)))
    near = jnp.concatenate([swapped, near], axis=2)
    got = spread_over(jnp.concatenate([tiles[0], corner], axis=1), "z", 8)
    head = got[0, :, :PW].astype(F32)
    parts = got[:, :, PW:].astype(F32)
    parts = parts[:, :8, :T] + parts[:, 8:, :T] + parts[:, :8, T:]
    sent = jnp.concatenate([head[:8], head[8:]] + [parts[z] for z in range(8)], axis=1)
    own = spread_over(sent, ("x", "y"), 16).reshape(4, 4, 8, 4 * PW)
    other = lax.ppermute(own, AXES, moves(lambda r, y, z: (r ^ 1, y, z)))
    near = spread_over(near, ("x", "core"), 8)
    inv, first = block(core, own, other)
    updated, panel_t = last(normal, wide, *far(col, inv, first, near))
    return updated, panel_t.T


def solution(mesh):
    fine = Mesh(mesh.devices.reshape(4, 2, 4, 8), AXES)
    rows, cols = ("x", "core"), ("y", "z")
    return jax.shard_map(
        per_device,
        mesh=fine,
        in_specs=(P(rows, cols), P(None, AXES)),
        out_specs=(P(rows, cols), P(rows, cols)),
        check_vma=False,
    )
```

```python
import functools

import jax
import jax.numpy as jnp
from jax import lax
from jax.experimental import pallas as pl
from jax.experimental.pallas import tpu as pltpu
from jax.sharding import Mesh
from jax.sharding import PartitionSpec as P

PW = 512
NB = 16
T = 128
AXES = ("x", "core", "y", "z")
F32 = jnp.float32
BF16 = jnp.bfloat16
HI = lax.Precision.HIGHEST
VMEM = pltpu.VMEM


def nt(a, b, precision=None):
    return lax.dot_general(a, b, (((1,), (1,)), ((), ())), precision=precision, preferred_element_type=F32)


def nn(a, b, precision=None):
    return lax.dot_general(a, b, (((1,), (0,)), ((), ())), precision=precision, preferred_element_type=F32)


def tn(a, b):
    return lax.dot_general(a, b, (((0,), (0,)), ((), ())), preferred_element_type=F32)


def in_vmem(x):
    return pltpu.with_memory_space_constraint(x, pltpu.VMEM)


def in_hbm(x):
    return pltpu.with_memory_space_constraint(x, pltpu.HBM)


def split(x):
    high = x.astype(BF16)
    return high, (x - high.astype(F32)).astype(BF16)


def wide_kernel(cols_ref, jac_ref, wide_ref):
    high, low = split(cols_ref[...].T[:NB])
    for q in range(2):
        wide_ref[0, q] = high[:, q * PW : (q + 1) * PW]
        wide_ref[1, q] = low[:, q * PW : (q + 1) * PW]
        wide_ref[2, q] = jac_ref[q * NB : (q + 1) * NB, :]


def prep_wide(normal, jac_t):
    rows = normal.shape[0]
    parts = pl.pallas_call(
        wide_kernel,
        grid=(2,),
        in_specs=[
            pl.BlockSpec((rows // 2, T), lambda i: (i, 0)),
            pl.BlockSpec((2 * NB, PW), lambda i: (i, 0)),
        ],
        out_specs=pl.BlockSpec((3, 2, NB, PW), lambda i: (0, i, 0, 0)),
        out_shape=jax.ShapeDtypeStruct((3, 4, NB, PW), BF16),
        compiler_params=pltpu.CompilerParams(vmem_limit_bytes=62 << 20),
    )(normal, jac_t)
    return parts.reshape(12, NB, PW)


def near_kernel(rows_ref, corner_ref, near_ref):
    cols = rows_ref[:, :T].T[:NB]
    corner = jnp.concatenate([cols[:8], cols[8:]], axis=1)
    first = corner.astype(BF16).astype(F32)
    second = (corner - first).astype(BF16).astype(F32)
    third = corner - first - second
    corner_ref[:, :T] = jnp.concatenate([first, second], axis=0).astype(BF16)
    corner_ref[:, T:] = jnp.concatenate([third, third], axis=0).astype(BF16)
    high, low = split(rows_ref[...])
    for i in range(4):
        near_ref[i, :, :PW] = high[i * NB : (i + 1) * NB]
        near_ref[i, :, PW:] = low[i * NB : (i + 1) * NB]


def prep_near(normal):
    return pl.pallas_call(
        near_kernel,
        grid=(1,),
        in_specs=[pl.BlockSpec((64, PW), lambda i: (0, 0))],
        out_specs=[
            pl.BlockSpec((NB, 2 * T), lambda i: (0, 0)),
            pl.BlockSpec((4, NB, 2 * PW), lambda i: (0, 0, 0)),
        ],
        out_shape=[
            jax.ShapeDtypeStruct((NB, 2 * T), BF16),
            jax.ShapeDtypeStruct((4, NB, 2 * PW), BF16),
        ],
        compiler_params=pltpu.CompilerParams(vmem_limit_bytes=62 << 20),
    )(normal)


def factor_tile(tile):
    q = 8
    groups = T // q
    rows = [tile[q * i : q * (i + 1), :] for i in range(groups)]
    lane = lax.broadcasted_iota(jnp.int32, (q, T), 1)
    out = []
    spread = lambda v: jnp.broadcast_to(v, (q, T))
    for g in range(groups):
        base = g * q
        cols = {i: [spread(rows[i][:, base + l : base + l + 1]) for l in range(q)] for i in range(g, groups)}
        low = [[None] * q for _ in range(q)]
        r = [None] * q
        pivot = [[spread(cols[g][l][k : k + 1, :]) if k >= l else None for l in range(q)] for k in range(q)]
        inside = (lane >= base) & (lane < base + q)
        done = [
            jnp.where(inside, jnp.where(lane == base + l, 1.0, 0.0), spread(rows[g][l : l + 1, :])) for l in range(q)
        ]
        near = list(cols[g + 1]) if g + 1 < groups else None
        for j in range(q):
            r[j] = lax.rsqrt(pivot[j][j])
            done[j] = done[j] * r[j]
            for i in range(j + 1, q):
                low[i][j] = pivot[i][j] * r[j]
            for i in range(j + 1, q):
                for k in range(j + 1, i + 1):
                    pivot[i][k] = pivot[i][k] - low[i][j] * low[k][j]
                done[i] = done[i] - low[i][j] * done[j]
            if near:
                near[j] = near[j] * r[j]
                for k in range(j + 1, q):
                    near[k] = near[k] - low[k][j] * near[j]
        weight = list(done)
        for j in range(q - 1, -1, -1):
            weight[j] = weight[j] * r[j]
            for i in range(j):
                weight[i] = weight[i] - low[j][i] * weight[j]
        sub = lax.broadcasted_iota(jnp.int32, (q, T), 0)
        mine = done[0]
        for k in range(1, q):
            mine = jnp.where(sub >= k, done[k], mine)
        out.append(jnp.where(lane < base + q, mine, 0.0))
        for i in range(g + 1, groups):
            left, right = (near, done) if i == g + 1 else (cols[i], weight)
            acc = left[0] * right[0]
            for k in range(1, q):
                acc = acc + left[k] * right[k]
            rows[i] = jnp.where(inside, 0.0, rows[i]) - acc
    return jnp.concatenate(out, 0)


def factor(work, inv):
    inv[...] = jnp.zeros_like(inv)
    tiles = PW // T
    for b in range(tiles):
        lo, hi = b * T, (b + 1) * T
        here = factor_tile(work[lo:hi, lo:hi])
        inv[lo:hi, lo:hi] = here
        if b:
            inv[lo:hi, :lo] = nn(here, inv[lo:hi, :lo], HI)
        if b < tiles - 1:
            below = nt(work[hi:, lo:hi], here, HI)
            work[hi : hi + T, hi : hi + T] -= nt(below[:T], below[:T], HI)
            if b < tiles - 2:
                work[hi + T :, hi:] -= nt(below[T:], below, HI)
            inv[hi:, :hi] -= nn(below, inv[lo:hi, :hi], HI)


def place(refs, core, store):
    for x in range(4):
        for ref, r in ((refs[0], 2 * x + core), (refs[1], 2 * x + 1 - core)):
            for a in range(4):
                store(ref, x, a, r)


def tile_rows(a, r):
    return pl.ds(pl.multiple_of(a * T + r * NB, NB), NB)


def block_kernel(core_ref, own_ref, other_ref, inv_ref, first_ref, work, pieces):
    core = core_ref[0]

    def store(ref, x, a, r):
        upper, lower = ref[x, a, :, :PW], ref[x, a, :, PW : 2 * PW]
        first_ref[tile_rows(a, r), :] = jnp.concatenate([upper, lower], axis=0).astype(BF16)
        lanes = pl.ds(pl.multiple_of(r * T, T), T)
        for z in range(8):
            start = 2 * PW + z * T
            pieces[(a * 8 + z) * 8 : (a * 8 + z + 1) * 8, lanes] = ref[x, a, :, start : start + T]

    place((own_ref, other_ref), core, store)
    src = lax.broadcasted_iota(jnp.int32, (8 * T, PW), 0)
    dst = lax.broadcasted_iota(jnp.int32, (8 * T, PW), 1)
    to = (src // 16 % 4) * T + (src // T) * NB + src % NB
    high, rest = split(pieces[...])
    rest = pieces[...] - high.astype(F32)
    middle, low = split(rest)
    for half in range(2):
        move = jnp.where((to == dst) & (src // 64 % 2 == half), 1.0, 0.0).astype(BF16)
        part = nn(high, move) + nn(middle, move) + nn(low, move)
        work.reshape(32, 2, 8, PW)[:, half] = part.reshape(32, 8, PW)
    first = first_ref[...]
    work[...] += nt(first, first)
    factor(work, inv_ref)


def block(core, own, other):
    whole = pl.BlockSpec(memory_space=VMEM)
    return pl.pallas_call(
        block_kernel,
        in_specs=[pl.BlockSpec(memory_space=pltpu.SMEM), whole, whole],
        out_specs=[whole] * 2,
        out_shape=[VMEM((PW, PW), F32), jax.ShapeDtypeStruct((PW, PW), BF16)],
        scratch_shapes=[VMEM((PW, PW), F32), VMEM((256, 8 * T), F32)],
        compiler_params=pltpu.CompilerParams(vmem_limit_bytes=48 << 20),
    )(core, own, other)


def split3(x):
    high, rest = x.astype(BF16), x - x.astype(BF16).astype(F32)
    middle, low = split(rest)
    return high, middle, low


def far_kernel(col_ref, inv_ref, first_ref, near, w_hi, w_lo, v_hi, v_lo, own_rows, own_jac, cols, gram):
    for r in range(8):
        for a in range(4):
            at = slice(a * T + r * NB, a * T + (r + 1) * NB)
            cols[at, :] = near[r, a, :, :PW]
            gram[at, :] = near[r, a, :, PW : 2 * PW].astype(F32) + near[r, a, :, 2 * PW :].astype(F32)
    first = first_ref[...]
    inv = inv_ref[...]
    panel = nn(inv, gram[...] + nt(first, cols[...]), HI)
    weight = nn(inv.T, panel, HI)
    high, middle, low = split3(weight)
    w_hi[...] = high
    w_lo[...] = middle
    change = tn(high, first) + (tn(middle, first) + tn(low, first))
    high, low = split(cols[...].astype(F32) - change)
    v_hi[...] = high
    v_lo[...] = low
    mine = inv_ref[pl.ds(pl.multiple_of(col_ref[0] * NB, NB), NB), :]
    high, middle, low = split3(mine)
    own_rows[:NB, :] = high
    own_rows[NB:, :] = middle
    high, low = split(nn(high, first) + (nn(middle, first) + nn(low, first)))
    own_jac[:NB, :] = high
    own_jac[NB:, :] = low


def far(col, inv, first, near):
    whole = pl.BlockSpec(memory_space=VMEM)
    return pl.pallas_call(
        far_kernel,
        in_specs=[pl.BlockSpec(memory_space=pltpu.SMEM)] + [whole] * 3,
        out_specs=[whole] * 6,
        out_shape=[VMEM((PW, PW), BF16), jax.ShapeDtypeStruct((PW, PW), BF16)]
        + [VMEM((PW, PW), BF16)] * 2
        + [VMEM((2 * NB, PW), BF16)] * 2,
        scratch_shapes=[VMEM((PW, PW), BF16), VMEM((PW, PW), F32)],
        compiler_params=pltpu.CompilerParams(vmem_limit_bytes=48 << 20),
    )(col, in_vmem(inv), first, near)


def last_kernel(
    normal, wide, w_lo, w_hi, v_hi, v_lo, own_rows, own_jac, out, panel_out,
    wide_in, normal_in, w_lo_in, out_buf, sem, sem_w, sem_out,
):
    chunks = []
    for q in range(4):
        jac = pl.ds(8 * q, 8), pl.ds(8, 4)
        rows = pl.ds(q * PW, PW)
        chunks.append(
            [
                pltpu.make_async_copy(wide.at[jac], wide_in.at[jac], sem.at[q, 0]),
                pltpu.make_async_copy(wide.at[:, q], wide_in.at[:, q], sem.at[q, 1]),
                pltpu.make_async_copy(wide.at[:, 4 + q], wide_in.at[:, 4 + q], sem.at[q, 2]),
                pltpu.make_async_copy(normal.at[rows], normal_in.at[rows], sem.at[q, 3]),
            ]
        )
    copy_w = pltpu.make_async_copy(w_lo, w_lo_in, sem_w)
    for copy in chunks[0][:3] + [copy_w] + chunks[0][3:]:
        copy.start()
    moves_out = []
    for q in range(4):
        rows = slice(q * PW, (q + 1) * PW)
        chunks[q][0].wait()
        jac_rows = wide_in[8 * q : 8 * q + 8, 8:12].reshape(PW, PW)
        sums = nt(jac_rows, v_hi[...]) + nt(jac_rows, v_lo[...])
        mine = nt(own_jac[...], jac_rows)
        for copy in chunks[q][1:] + [copy_w] * (q == 0):
            copy.wait()
        if q < 3:
            for copy in chunks[q + 1]:
                copy.start()
        high = wide_in[:, q].reshape(PW, PW)
        low = wide_in[:, 4 + q].reshape(PW, PW)
        drop = tn(high, w_hi[...]) + (tn(low, w_hi[...]) + tn(high, w_lo_in[...]))
        out_buf[rows, :] = normal_in[rows, :] + (sums - drop)
        moves_out.append(
            pltpu.make_async_copy(out_buf.at[pl.ds(q * PW, PW)], out.at[pl.ds(q * PW, PW)], sem_out.at[q])
        )
        moves_out[q].start()
        mine = mine + nn(own_rows[...], high)
        panel_out[:, rows] = mine[:NB] + mine[NB:] + nn(own_rows[:NB], low)
    for copy in moves_out:
        copy.wait()


def last(normal, wide, w_hi, w_lo, *parts):
    rows = normal.shape[0]
    there = pl.BlockSpec(memory_space=pl.ANY)
    whole = pl.BlockSpec(memory_space=VMEM)
    return pl.pallas_call(
        last_kernel,
        in_specs=[there] * 3 + [whole] * 5,
        out_specs=[there, whole],
        out_shape=[
            jax.ShapeDtypeStruct((rows, PW), F32),
            jax.ShapeDtypeStruct((NB, rows), F32),
        ],
        scratch_shapes=[
            VMEM((32, 12, NB, PW), BF16),
            VMEM((rows, PW), F32),
            VMEM((PW, PW), BF16),
            VMEM((rows, PW), F32),
            pltpu.SemaphoreType.DMA((4, 4)),
            pltpu.SemaphoreType.DMA,
            pltpu.SemaphoreType.DMA((4,)),
        ],
        compiler_params=pltpu.CompilerParams(vmem_limit_bytes=48 << 20),
    )(in_hbm(normal), in_hbm(wide), in_hbm(w_lo), in_vmem(w_hi), *(in_vmem(part) for part in parts))


def position(r, y, z):
    return (r * 4 + y) * 8 + z


def spread_over(value, axis, count):
    return lax.all_to_all(jnp.broadcast_to(value[None], (count,) + value.shape), axis, 0, 0, tiled=True)


def moves(to):
    return [(position(r, y, z), position(*to(r, y, z))) for r in range(8) for y in range(4) for z in range(8)]


def per_device(normal, jacobian):
    core = lax.axis_index("core").astype(jnp.int32)[None]
    col = (lax.axis_index("y") * 8 + lax.axis_index("z")).astype(jnp.int32)[None]
    jac_t = jacobian.T
    wide = prep_wide(normal, jac_t)
    wide = lax.all_gather(wide, ("y", "z"), axis=0, tiled=False)
    corner, near = prep_near(normal)
    tiles = lax.all_to_all(jac_t.reshape(4, NB, PW), "y", 0, 0, tiled=True)
    swapped = lax.ppermute(tiles, AXES, moves(lambda r, y, z: (z, y, r)))
    near = jnp.concatenate([swapped, near], axis=2)
    got = spread_over(jnp.concatenate([tiles[0], corner], axis=1), "z", 8)
    head = got[0, :, :PW].astype(F32)
    parts = got[:, :, PW:].astype(F32)
    parts = parts[:, :8, :T] + parts[:, 8:, :T] + parts[:, :8, T:]
    sent = jnp.concatenate([head[:8], head[8:]] + [parts[z] for z in range(8)], axis=1)
    own = spread_over(sent, ("x", "y"), 16).reshape(4, 4, 8, 4 * PW)
    other = lax.ppermute(own, AXES, moves(lambda r, y, z: (r ^ 1, y, z)))
    near = spread_over(near, ("x", "core"), 8)
    inv, first = block(core, own, other)
    updated, panel_t = last(normal, wide, *far(col, inv, first, near))
    return updated, panel_t.T


def solution(mesh):
    fine = Mesh(mesh.devices.reshape(4, 2, 4, 8), AXES)
    rows, cols = ("x", "core"), ("y", "z")
    return jax.shard_map(
        per_device,
        mesh=fine,
        in_specs=(P(rows, cols), P(None, AXES)),
        out_specs=(P(rows, cols), P(rows, cols)),
        check_vma=False,
    )
```

```python
import functools

import jax
import jax.numpy as jnp
from jax import lax
from jax.experimental import pallas as pl
from jax.experimental.pallas import tpu as pltpu
from jax.sharding import Mesh
from jax.sharding import PartitionSpec as P

PW = 512
NB = 16
T = 128
AXES = ("x", "core", "y", "z")
F32 = jnp.float32
BF16 = jnp.bfloat16
HI = lax.Precision.HIGHEST
VMEM = pltpu.VMEM


def nt(a, b, precision=None):
    return lax.dot_general(a, b, (((1,), (1,)), ((), ())), precision=precision, preferred_element_type=F32)


def nn(a, b, precision=None):
    return lax.dot_general(a, b, (((1,), (0,)), ((), ())), precision=precision, preferred_element_type=F32)


def tn(a, b):
    return lax.dot_general(a, b, (((0,), (0,)), ((), ())), preferred_element_type=F32)


def in_vmem(x):
    return pltpu.with_memory_space_constraint(x, pltpu.VMEM)


def in_hbm(x):
    return pltpu.with_memory_space_constraint(x, pltpu.HBM)


def split(x):
    high = x.astype(BF16)
    return high, (x - high.astype(F32)).astype(BF16)


def prep_kernel(cols_ref, rows_ref, jac_ref, wide_ref, corner_ref, near_ref):
    cols = cols_ref[...].T[:NB]
    high, low = split(cols)
    for q in range(4):
        wide_ref[q] = high[:, q * PW : (q + 1) * PW]
        wide_ref[4 + q] = low[:, q * PW : (q + 1) * PW]
        wide_ref[8 + q] = jac_ref[q * NB : (q + 1) * NB, :]
    corner = jnp.concatenate([cols[:8, :64], cols[8:, :64]], axis=1)
    first = corner.astype(BF16).astype(F32)
    second = (corner - first).astype(BF16).astype(F32)
    third = corner - first - second
    corner_ref[:, :T] = jnp.concatenate([first, second], axis=0).astype(BF16)
    corner_ref[:, T:] = jnp.concatenate([third, third], axis=0).astype(BF16)
    high, low = split(rows_ref[...])
    for i in range(4):
        near_ref[i, :, :PW] = high[i * NB : (i + 1) * NB]
        near_ref[i, :, PW:] = low[i * NB : (i + 1) * NB]


def prep(normal, jac_t):
    rows = normal.shape[0]
    return pl.pallas_call(
        prep_kernel,
        grid=(1,),
        in_specs=[
            pl.BlockSpec((rows, T), lambda i: (0, 0)),
            pl.BlockSpec((64, PW), lambda i: (0, 0)),
            pl.BlockSpec((64, PW), lambda i: (0, 0)),
        ],
        out_specs=[
            pl.BlockSpec((12, NB, PW), lambda i: (0, 0, 0)),
            pl.BlockSpec((NB, 2 * T), lambda i: (0, 0)),
            pl.BlockSpec((4, NB, 2 * PW), lambda i: (0, 0, 0)),
        ],
        out_shape=[
            jax.ShapeDtypeStruct((12, NB, PW), BF16),
            jax.ShapeDtypeStruct((NB, 2 * T), BF16),
            jax.ShapeDtypeStruct((4, NB, 2 * PW), BF16),
        ],
        compiler_params=pltpu.CompilerParams(vmem_limit_bytes=62 << 20),
    )(normal, normal, jac_t)


def factor_tile(tile):
    q = 8
    groups = T // q
    rows = [tile[q * i : q * (i + 1), :] for i in range(groups)]
    lane = lax.broadcasted_iota(jnp.int32, (q, T), 1)
    out = []
    spread = lambda v: jnp.broadcast_to(v, (q, T))
    for g in range(groups):
        base = g * q
        cols = {i: [spread(rows[i][:, base + l : base + l + 1]) for l in range(q)] for i in range(g, groups)}
        low = [[None] * q for _ in range(q)]
        r = [None] * q
        pivot = [[spread(cols[g][l][k : k + 1, :]) if k >= l else None for l in range(q)] for k in range(q)]
        inside = (lane >= base) & (lane < base + q)
        done = [
            jnp.where(inside, jnp.where(lane == base + l, 1.0, 0.0), spread(rows[g][l : l + 1, :])) for l in range(q)
        ]
        near = list(cols[g + 1]) if g + 1 < groups else None
        for j in range(q):
            r[j] = lax.rsqrt(pivot[j][j])
            done[j] = done[j] * r[j]
            for i in range(j + 1, q):
                low[i][j] = pivot[i][j] * r[j]
            for i in range(j + 1, q):
                for k in range(j + 1, i + 1):
                    pivot[i][k] = pivot[i][k] - low[i][j] * low[k][j]
                done[i] = done[i] - low[i][j] * done[j]
            if near:
                near[j] = near[j] * r[j]
                for k in range(j + 1, q):
                    near[k] = near[k] - low[k][j] * near[j]
        weight = list(done)
        for j in range(q - 1, -1, -1):
            weight[j] = weight[j] * r[j]
            for i in range(j):
                weight[i] = weight[i] - low[j][i] * weight[j]
        sub = lax.broadcasted_iota(jnp.int32, (q, T), 0)
        mine = done[0]
        for k in range(1, q):
            mine = jnp.where(sub >= k, done[k], mine)
        out.append(jnp.where(lane < base + q, mine, 0.0))
        for i in range(g + 1, groups):
            left, right = (near, done) if i == g + 1 else (cols[i], weight)
            acc = left[0] * right[0]
            for k in range(1, q):
                acc = acc + left[k] * right[k]
            rows[i] = jnp.where(inside, 0.0, rows[i]) - acc
    return jnp.concatenate(out, 0)


def factor(work, inv):
    inv[...] = jnp.zeros_like(inv)
    tiles = PW // T
    for b in range(tiles):
        lo, hi = b * T, (b + 1) * T
        here = factor_tile(work[lo:hi, lo:hi])
        inv[lo:hi, lo:hi] = here
        if b:
            inv[lo:hi, :lo] = nn(here, inv[lo:hi, :lo], HI)
        if b < tiles - 1:
            below = nt(work[hi:, lo:hi], here, HI)
            work[hi : hi + T, hi : hi + T] -= nt(below[:T], below[:T], HI)
            if b < tiles - 2:
                work[hi + T :, hi:] -= nt(below[T:], below, HI)
            inv[hi:, :hi] -= nn(below, inv[lo:hi, :hi], HI)


def place(refs, core, store):
    for x in range(4):
        for ref, r in ((refs[0], 2 * x + core), (refs[1], 2 * x + 1 - core)):
            for a in range(4):
                store(ref, x, a, r)


def tile_rows(a, r):
    return pl.ds(pl.multiple_of(a * T + r * NB, NB), NB)


def block_kernel(core_ref, own_ref, other_ref, inv_ref, first_ref, work, pieces):
    core = core_ref[0]

    def store(ref, x, a, r):
        upper, lower = ref[x, a, :, :PW], ref[x, a, :, PW : 2 * PW]
        first_ref[tile_rows(a, r), :] = jnp.concatenate([upper, lower], axis=0).astype(BF16)
        lanes = pl.ds(pl.multiple_of(r * T, T), T)
        for z in range(8):
            start = 2 * PW + z * T
            pieces[(a * 8 + z) * 8 : (a * 8 + z + 1) * 8, lanes] = ref[x, a, :, start : start + T]

    place((own_ref, other_ref), core, store)
    src = lax.broadcasted_iota(jnp.int32, (8 * T, PW), 0)
    dst = lax.broadcasted_iota(jnp.int32, (8 * T, PW), 1)
    to = (src // 16 % 4) * T + (src // T) * NB + src % NB
    high, rest = split(pieces[...])
    rest = pieces[...] - high.astype(F32)
    middle, low = split(rest)
    for half in range(2):
        move = jnp.where((to == dst) & (src // 64 % 2 == half), 1.0, 0.0).astype(BF16)
        part = nn(high, move) + nn(middle, move) + nn(low, move)
        work.reshape(32, 2, 8, PW)[:, half] = part.reshape(32, 8, PW)
    first = first_ref[...]
    work[...] += nt(first, first)
    factor(work, inv_ref)


def block(core, own, other):
    whole = pl.BlockSpec(memory_space=VMEM)
    return pl.pallas_call(
        block_kernel,
        in_specs=[pl.BlockSpec(memory_space=pltpu.SMEM), whole, whole],
        out_specs=[whole] * 2,
        out_shape=[VMEM((PW, PW), F32), jax.ShapeDtypeStruct((PW, PW), BF16)],
        scratch_shapes=[VMEM((PW, PW), F32), VMEM((256, 8 * T), F32)],
        compiler_params=pltpu.CompilerParams(vmem_limit_bytes=48 << 20),
    )(core, own, other)


def split3(x):
    high, rest = x.astype(BF16), x - x.astype(BF16).astype(F32)
    middle, low = split(rest)
    return high, middle, low


def far_kernel(col_ref, inv_ref, first_ref, near, w_hi, w_lo, v_hi, v_lo, own_rows, own_jac, cols, gram):
    for r in range(8):
        for a in range(4):
            at = slice(a * T + r * NB, a * T + (r + 1) * NB)
            cols[at, :] = near[r, a, :, :PW]
            gram[at, :] = near[r, a, :, PW : 2 * PW].astype(F32) + near[r, a, :, 2 * PW :].astype(F32)
    first = first_ref[...]
    inv = inv_ref[...]
    panel = nn(inv, gram[...] + nt(first, cols[...]), HI)
    weight = nn(inv.T, panel, HI)
    high, middle, low = split3(weight)
    w_hi[...] = high
    w_lo[...] = middle
    change = tn(high, first) + (tn(middle, first) + tn(low, first))
    high, low = split(cols[...].astype(F32) - change)
    v_hi[...] = high
    v_lo[...] = low
    mine = inv_ref[pl.ds(pl.multiple_of(col_ref[0] * NB, NB), NB), :]
    high, middle, low = split3(mine)
    own_rows[:NB, :] = high
    own_rows[NB:, :] = middle
    high, low = split(nn(high, first) + (nn(middle, first) + nn(low, first)))
    own_jac[:NB, :] = high
    own_jac[NB:, :] = low


def far(col, inv, first, near):
    whole = pl.BlockSpec(memory_space=VMEM)
    return pl.pallas_call(
        far_kernel,
        in_specs=[pl.BlockSpec(memory_space=pltpu.SMEM)] + [whole] * 3,
        out_specs=[whole] * 6,
        out_shape=[VMEM((PW, PW), BF16), jax.ShapeDtypeStruct((PW, PW), BF16)]
        + [VMEM((PW, PW), BF16)] * 2
        + [VMEM((2 * NB, PW), BF16)] * 2,
        scratch_shapes=[VMEM((PW, PW), BF16), VMEM((PW, PW), F32)],
        compiler_params=pltpu.CompilerParams(vmem_limit_bytes=48 << 20),
    )(col, in_vmem(inv), first, near)


def last_kernel(
    normal, wide, w_lo, w_hi, v_hi, v_lo, own_rows, own_jac, out, panel_out,
    wide_in, normal_in, w_lo_in, out_buf, sem, sem_w, sem_out,
):
    chunks = []
    for q in range(4):
        jac = pl.ds(8 * q, 8), pl.ds(8, 4)
        rows = pl.ds(q * PW, PW)
        chunks.append(
            [
                pltpu.make_async_copy(wide.at[jac], wide_in.at[jac], sem.at[q, 0]),
                pltpu.make_async_copy(wide.at[:, q], wide_in.at[:, q], sem.at[q, 1]),
                pltpu.make_async_copy(wide.at[:, 4 + q], wide_in.at[:, 4 + q], sem.at[q, 2]),
                pltpu.make_async_copy(normal.at[rows], normal_in.at[rows], sem.at[q, 3]),
            ]
        )
    copy_w = pltpu.make_async_copy(w_lo, w_lo_in, sem_w)
    for copy in chunks[0][:3] + [copy_w] + chunks[0][3:]:
        copy.start()
    moves_out = []
    for q in range(4):
        rows = slice(q * PW, (q + 1) * PW)
        chunks[q][0].wait()
        if q < 3:
            for copy in chunks[q + 1]:
                copy.start()
        jac_rows = wide_in[8 * q : 8 * q + 8, 8:12].reshape(PW, PW)
        sums = nt(jac_rows, v_hi[...]) + nt(jac_rows, v_lo[...])
        mine = nt(own_jac[...], jac_rows)
        for copy in chunks[q][1:] + [copy_w] * (q == 0):
            copy.wait()
        high = wide_in[:, q].reshape(PW, PW)
        low = wide_in[:, 4 + q].reshape(PW, PW)
        drop = tn(high, w_hi[...]) + (tn(low, w_hi[...]) + tn(high, w_lo_in[...]))
        out_buf[rows, :] = normal_in[rows, :] + (sums - drop)
        moves_out.append(
            pltpu.make_async_copy(out_buf.at[pl.ds(q * PW, PW)], out.at[pl.ds(q * PW, PW)], sem_out.at[q])
        )
        moves_out[q].start()
        mine = mine + nn(own_rows[...], high)
        panel_out[:, rows] = mine[:NB] + mine[NB:] + nn(own_rows[:NB], low)
    for copy in moves_out:
        copy.wait()


def last(normal, wide, w_hi, w_lo, *parts):
    rows = normal.shape[0]
    there = pl.BlockSpec(memory_space=pl.ANY)
    whole = pl.BlockSpec(memory_space=VMEM)
    return pl.pallas_call(
        last_kernel,
        in_specs=[there] * 3 + [whole] * 5,
        out_specs=[there, whole],
        out_shape=[
            jax.ShapeDtypeStruct((rows, PW), F32),
            jax.ShapeDtypeStruct((NB, rows), F32),
        ],
        scratch_shapes=[
            VMEM((32, 12, NB, PW), BF16),
            VMEM((rows, PW), F32),
            VMEM((PW, PW), BF16),
            VMEM((rows, PW), F32),
            pltpu.SemaphoreType.DMA((4, 4)),
            pltpu.SemaphoreType.DMA,
            pltpu.SemaphoreType.DMA((4,)),
        ],
        compiler_params=pltpu.CompilerParams(vmem_limit_bytes=48 << 20),
    )(in_hbm(normal), in_hbm(wide), in_hbm(w_lo), in_vmem(w_hi), *(in_vmem(part) for part in parts))


def position(r, y, z):
    return (r * 4 + y) * 8 + z


def spread_over(value, axis, count):
    return lax.all_to_all(jnp.broadcast_to(value[None], (count,) + value.shape), axis, 0, 0, tiled=True)


def moves(to):
    return [(position(r, y, z), position(*to(r, y, z))) for r in range(8) for y in range(4) for z in range(8)]


def per_device(normal, jacobian):
    core = lax.axis_index("core").astype(jnp.int32)[None]
    col = (lax.axis_index("y") * 8 + lax.axis_index("z")).astype(jnp.int32)[None]
    jac_t = jacobian.T
    wide, corner, near = prep(normal, jac_t)
    wide = lax.all_gather(wide, ("y", "z"), axis=0, tiled=False)
    tiles = lax.all_to_all(jac_t.reshape(4, NB, PW), "y", 0, 0, tiled=True)
    swapped = lax.ppermute(tiles, AXES, moves(lambda r, y, z: (z, y, r)))
    near = jnp.concatenate([swapped, near], axis=2)
    got = spread_over(jnp.concatenate([tiles[0], corner], axis=1), "z", 8)
    head = got[0, :, :PW].astype(F32)
    parts = got[:, :, PW:].astype(F32)
    parts = parts[:, :8, :T] + parts[:, 8:, :T] + parts[:, :8, T:]
    sent = jnp.concatenate([head[:8], head[8:]] + [parts[z] for z in range(8)], axis=1)
    own = spread_over(sent, ("x", "y"), 16).reshape(4, 4, 8, 4 * PW)
    other = lax.ppermute(own, AXES, moves(lambda r, y, z: (r ^ 1, y, z)))
    near = spread_over(near, ("x", "core"), 8)
    inv, first = block(core, own, other)
    updated, panel_t = last(normal, wide, *far(col, inv, first, near))
    return updated, panel_t.T


def solution(mesh):
    fine = Mesh(mesh.devices.reshape(4, 2, 4, 8), AXES)
    rows, cols = ("x", "core"), ("y", "z")
    return jax.shard_map(
        per_device,
        mesh=fine,
        in_specs=(P(rows, cols), P(None, AXES)),
        out_specs=(P(rows, cols), P(rows, cols)),
        check_vma=False,
    )
```
